512 devices in a mesh: row: 16 (over x, y), col: 32 (over z, core).
Axes of the slice: x: 4, y: 4, z: 16, core: 2. Of those that a mesh axis runs over, the one named last changes fastest.
Arguments:
- field: bfloat16 [384, 256, 1024], P('row', 'col'), may hold values from -6 to 6
- mix: bfloat16 [1024, 1024], replicated, may hold values from -0.1875 to 0.1875
- stencil: float32 [2, 3, 3], replicated, may hold values from -2.5 to 2.5
- spectral: float32 [2, 8, 8, 1024], replicated, may hold values from -2.5 to 2.5
- cotangent: bfloat16 [384, 256, 1024], P('row', 'col'), may hold values from -6 to 6
Outputs:
- layer_out: bfloat16 [384, 256, 1024], P('row', 'col')
- grad_field: bfloat16 [384, 256, 1024], P('row', 'col')
The draws below stay inside these ranges and needn't reach their ends.
All inputs are finite; a program needn't handle non-finite values.
Results may differ from the reference program's by a relative error of at most 0.0055.
The reference program's roundings to bfloat16 on the way count: a program that leaves them out, or rounds other values in their place, can miss the bound.
Values may be sent and summed in bfloat16 or wider, within the bound.
No kernel may reach another device: no remote copies, remote signals or barrier semaphores. Data moves between devices by JAX's collectives and lax.ppermute only.
A program may use at most 64 MiB of HBM per device.

```python
import math
import jax
import jax.numpy as jnp
import numpy as np
from jax import lax

CH = 64
K = 4
LEVELS = 2
MODES = 8
F = 1024
NR = 384
NC = 256


def steps_of(own_key, extent, split, low, largest):
    gain = 1.0
    for axis_at, blocks in split:
        draws = jax.random.uniform(jax.random.fold_in(jax.random.fold_in(own_key, 6), axis_at), (blocks,), jnp.float32, low / len(split), largest / len(split))
        gain = gain * jnp.repeat(jnp.exp(draws), extent[axis_at] // blocks).reshape((-1,) + (1,) * (len(extent) - 1 - axis_at))
    return gain


def bell_draw(own_key, extent, deviation, limit, shards=(), kind=jnp.bfloat16):
    result = jax.random.normal(own_key, extent, jnp.float32) * deviation
    if len(shards) > 0:
        result = steps_of(own_key, extent, shards, -0.22, 0.18) * result
    return jnp.clip(result, min=-limit, max=limit).astype(kind)


def setup_inputs(seed: int = 0) -> dict:
    key_list = jax.random.split(jax.random.key(seed), 6)
    field = bell_draw(key_list[0], (NR, NC, F), 1.0, 6.0, ((0, 16), (1, 32)))
    mix = bell_draw(key_list[1], (F, F), F ** -0.5, 0.1875)
    stencil = bell_draw(key_list[2], (LEVELS, 3, 3), 0.35, 2.5, (), jnp.float32)
    spectral = bell_draw(key_list[3], (2, MODES, MODES, F), 0.25, 2.5, (), jnp.float32)
    cotangent = bell_draw(key_list[4], (NR, NC, F), 1.0, 6.0, ((0, 16), (1, 32)))
    return dict(field=field, mix=mix, stencil=stencil, spectral=spectral, cotangent=cotangent)


def shifted_legendre(order_count):
    length = order_count + 1
    polys = [np.zeros(length), np.zeros(length)]
    polys[0][0] = 1.0
    polys[1][0] = -1.0
    polys[1][1] = 2.0
    for degree in range(1, order_count):
        times_t = np.zeros(length)
        times_t[1:] = 2.0 * polys[degree][:-1]
        times_t = times_t - polys[degree]
        polys.append(((2.0 * degree + 1.0) * times_t - degree * polys[degree - 1]) / (degree + 1.0))
    return [np.sqrt(2.0 * degree + 1.0) * polys[degree] for degree in range(order_count)]

def integrate_product(first, second):
    total = 0.0
    for power_a in range(first.shape[0]):
        for power_b in range(second.shape[0]):
            total = total + first[power_a] * second[power_b] / (power_a + power_b + 1.0)
    return total

def two_scale(order_count):
    polys = shifted_legendre(order_count)
    length = polys[0].shape[0]
    left_half = np.zeros((order_count, order_count))
    right_half = np.zeros((order_count, order_count))
    for out_index in range(order_count):
        coeffs = polys[out_index]
        halved = np.array([coeffs[power] * 0.5 ** power for power in range(length)])
        moved = np.zeros(length)
        for power in range(length):
            for lower in range(power + 1):
                moved[lower] = moved[lower] + coeffs[power] * 0.5 ** power * math.comb(power, lower)
        for in_index in range(order_count):
            left_half[out_index, in_index] = integrate_product(halved, polys[in_index]) / np.sqrt(2.0)
            right_half[out_index, in_index] = integrate_product(moved, polys[in_index]) / np.sqrt(2.0)
    scaling_rows = np.concatenate([left_half, right_half], axis=1)
    vectors = [scaling_rows[out_index] for out_index in range(order_count)]
    wavelet_rows = []
    for out_index in range(order_count):
        vector = np.zeros(2 * order_count)
        vector[out_index] = 1.0
        vector[order_count + out_index] = -1.0
        for earlier in vectors:
            vector = vector - np.dot(earlier, vector) * earlier
        vector = vector / np.sqrt(np.dot(vector, vector))
        vectors.append(vector)
        wavelet_rows.append(vector)
    filter_bank = np.stack([scaling_rows, np.stack(wavelet_rows)]).reshape(2, order_count, 2, order_count)
    return jnp.asarray(filter_bank, jnp.float32)

def decompose(state, filter_bank):
    height, breadth = (state.shape[0], state.shape[1])
    blocks = state.reshape(height // 2, 2, breadth // 2, 2, K, K, CH)
    parts = jnp.einsum('xmak,ynbl,iajbklc->ijxymnc', filter_bank, filter_bank, blocks, precision=lax.Precision.HIGHEST)
    parts = parts.reshape(height // 2, breadth // 2, 4, K * K * CH)
    return (parts[:, :, 0], parts[:, :, 1:])

def reconstruct(coarse, details, filter_bank):
    height, breadth = (coarse.shape[0], coarse.shape[1])
    parts = jnp.concatenate([coarse[:, :, None], details], axis=2).reshape(height, breadth, 2, 2, K, K, CH)
    blocks = jnp.einsum('xmak,ynbl,ijxymnc->iajbklc', filter_bank, filter_bank, parts, precision=lax.Precision.HIGHEST)
    return blocks.reshape(2 * height, 2 * breadth, K * K * CH)

def apply_taps(detail, taps, direction):
    total = jnp.zeros(detail.shape, jnp.float32)
    for shift_row in (-1, 0, 1):
        for shift_col in (-1, 0, 1):
            moved = jnp.roll(detail, (-direction * shift_row, -direction * shift_col), axis=(0, 1))
            total = total + taps[shift_row + 1, shift_col + 1] * moved
    return total

def mode_basis(row_start, col_start, rows_here, cols_here, rows_all, cols_all):
    row_pos = row_start + lax.iota(jnp.int32, rows_here)
    col_pos = col_start + lax.iota(jnp.int32, cols_here)
    freqs = lax.iota(jnp.int32, MODES)
    numer = (freqs[:, None, None, None] * row_pos[None, None, :, None] * cols_all + freqs[None, :, None, None] * col_pos[None, None, None, :] * rows_all) % (rows_all * cols_all)
    angles = numer.astype(jnp.float32) * (2.0 * math.pi / (rows_all * cols_all))
    return jnp.stack([jnp.cos(angles), jnp.sin(angles)]).reshape(2 * MODES * MODES, rows_here * cols_here)

def mix_detail(pre_act, mix):
    hidden = jax.nn.gelu(pre_act).astype(jnp.bfloat16)
    width = hidden.shape[-1]
    return jnp.dot(hidden.reshape(-1, width), mix, preferred_element_type=jnp.float32).reshape(pre_act.shape)

def reference(field, mix, stencil, spectral, cotangent):
    filter_bank = two_scale(K)
    width = field.shape[2]
    state = field.astype(jnp.float32)
    activations = []
    for level_index in range(LEVELS):
        state, detail = decompose(state, filter_bank)
        activations.append(apply_taps(detail.astype(jnp.bfloat16), stencil[level_index], 1))
    coarse_rows, coarse_cols = (state.shape[0], state.shape[1])
    basis = mode_basis(0, 0, coarse_rows, coarse_cols, coarse_rows, coarse_cols)
    scale = 1.0 / math.sqrt(coarse_rows * coarse_cols)
    gains = spectral.reshape(-1, width)
    modes = jnp.dot(basis, state.reshape(-1, width), precision=lax.Precision.HIGHEST) * scale
    upward = jnp.dot(basis.T, gains * modes, precision=lax.Precision.HIGHEST).reshape(coarse_rows, coarse_cols, width)
    for level_index in reversed(range(LEVELS)):
        upward = reconstruct(upward, mix_detail(activations[level_index], mix), filter_bank)
    layer_out = upward.astype(jnp.bfloat16)
    grad_state = cotangent.astype(jnp.float32)
    fines = []
    for level_index in range(LEVELS):
        grad_state, fine = decompose(grad_state, filter_bank)
        fines.append(fine.astype(jnp.bfloat16))
    back_modes = jnp.dot(basis, grad_state.reshape(-1, width), precision=lax.Precision.HIGHEST)
    downward = jnp.dot(basis.T, gains * back_modes, precision=lax.Precision.HIGHEST).reshape(coarse_rows, coarse_cols, width) * scale
    for level_index in reversed(range(LEVELS)):
        pre_act = activations[level_index]
        _, pullback = jax.vjp(jax.nn.gelu, pre_act)
        pre_grad = jnp.dot(fines[level_index].reshape(-1, width), mix.T, preferred_element_type=jnp.float32).reshape(pre_act.shape)
        act_grad = pullback(pre_grad)[0].astype(jnp.bfloat16)
        downward = reconstruct(downward, apply_taps(act_grad, stencil[level_index], -1), filter_bank)
    return (layer_out, downward.astype(jnp.bfloat16))
```

```python
import functools
import math

import jax
import jax.numpy as jnp
import ml_dtypes
import numpy as np
from jax import lax
from jax.experimental import pallas as pl
from jax.experimental.pallas import tpu as pltpu
from jax.sharding import PartitionSpec as P

CH = 64
K = 4
MODES = 8
F = 1024
BF = jnp.bfloat16
F32 = jnp.float32
QW = K * CH

FI, FJ = 24, 8
H1, W1 = 12, 4
H2, W2 = 6, 2
G1, G2 = 64, 16
SIDES = [(-1, 0), (1, 0), (0, -1), (0, 1)]


def shifted_legendre(order_count):
    length = order_count + 1
    polys = [np.zeros(length), np.zeros(length)]
    polys[0][0] = 1.0
    polys[1][0] = -1.0
    polys[1][1] = 2.0
    for degree in range(1, order_count):
        times_t = np.zeros(length)
        times_t[1:] = 2.0 * polys[degree][:-1]
        times_t = times_t - polys[degree]
        polys.append(((2.0 * degree + 1.0) * times_t - degree * polys[degree - 1]) / (degree + 1.0))
    return [np.sqrt(2.0 * degree + 1.0) * polys[degree] for degree in range(order_count)]


def integrate_product(first, second):
    total = 0.0
    for power_a in range(first.shape[0]):
        for power_b in range(second.shape[0]):
            total = total + first[power_a] * second[power_b] / (power_a + power_b + 1.0)
    return total


def two_scale(order_count):
    polys = shifted_legendre(order_count)
    length = polys[0].shape[0]
    left_half = np.zeros((order_count, order_count))
    right_half = np.zeros((order_count, order_count))
    for out_index in range(order_count):
        coeffs = polys[out_index]
        halved = np.array([coeffs[power] * 0.5**power for power in range(length)])
        moved = np.zeros(length)
        for power in range(length):
            for lower in range(power + 1):
                moved[lower] = moved[lower] + coeffs[power] * 0.5**power * math.comb(power, lower)
        for in_index in range(order_count):
            left_half[out_index, in_index] = integrate_product(halved, polys[in_index]) / np.sqrt(2.0)
            right_half[out_index, in_index] = integrate_product(moved, polys[in_index]) / np.sqrt(2.0)
    scaling_rows = np.concatenate([left_half, right_half], axis=1)
    vectors = [scaling_rows[out_index] for out_index in range(order_count)]
    wavelet_rows = []
    for out_index in range(order_count):
        vector = np.zeros(2 * order_count)
        vector[out_index] = 1.0
        vector[order_count + out_index] = -1.0
        for earlier in vectors:
            vector = vector - np.dot(earlier, vector) * earlier
        vector = vector / np.sqrt(np.dot(vector, vector))
        vectors.append(vector)
        wavelet_rows.append(vector)
    return np.stack([scaling_rows, np.stack(wavelet_rows)]).reshape(2, order_count, 2, order_count)


BANK = two_scale(K)
BANK[np.abs(BANK) < 1e-12] = 0.0


def halves(array):
    high = np.asarray(array, np.float32).astype(ml_dtypes.bfloat16)
    low = (np.asarray(array, np.float64) - high.astype(np.float64)).astype(ml_dtypes.bfloat16)
    return high, low


COL_FILTER = np.kron(BANK.transpose(2, 3, 0, 1).reshape(2 * K, 2 * K), np.eye(CH))


def rho(i, j):
    return ((i % 2) * 2 + j % 2) * G2 + (i // 2) * W2 + j // 2


def local_row(kind, i, j):
    if kind == "d1":
        return rho(i, j)
    if kind == "d2":
        return G1 + i * W2 + j
    if kind == "b1":
        return G1 + G2 + rho(i, j)
    return 2 * G1 + G2 + i * W2 + j


LOC = 2 * (G1 + G2)
REACH = {"d1": (H1, W1, 2), "d2": (H2, W2, 2), "b1": (H1, W1, 1), "b2": (H2, W2, 1)}


TWICE = np.einsum("pbm,mak->pbak", BANK[0], BANK[0]).reshape(K, 4, K)
COARSE_LEFT = np.zeros((K, 4, K, G2, FI * FJ))
for i_ in range(FI):
    for j_ in range(FJ):
        COARSE_LEFT[:, j_ % 4, :, (i_ // 4) * W2 + j_ // 4, i_ * FJ + j_] = TWICE[:, i_ % 4, :].T
COARSE_LEFT = COARSE_LEFT.reshape(K, 4 * K * G2, FI * FJ)
COARSE_RIGHT = np.kron(TWICE.transpose(1, 2, 0).reshape(4 * K, K), np.eye(CH))


def gather_table():
    table = np.zeros((4 * G1, FI * FJ), np.float32)
    for i in range(FI):
        for j in range(FJ):
            table[((i % 2) * 2 + j % 2) * G1 + rho(i // 2, j // 2), i * FJ + j] = 1.0
    return table


COLUMN = {}
for kind_, (height_, breadth_, _) in REACH.items():
    for i_ in range(height_):
        for j_ in range(breadth_):
            COLUMN[(kind_, i_, j_)] = local_row(kind_, i_, j_)


def message_plan():
    at, plan, starts = LOC, [], []
    for first in (0, 2):
        for dr, dc in SIDES[first : first + 2]:
            message = []
            for part in ("d", "b"):
                cells = []
                for kind, (height, breadth, reach) in REACH.items():
                    if kind[0] != part:
                        continue
                    rows, columns = range(-reach, height + reach), range(-reach, breadth + reach)
                    if dr:
                        rows = rows[:reach] if dr < 0 else rows[-reach:]
                        columns = columns[reach:-reach]
                    else:
                        columns = columns[:reach] if dc < 0 else columns[-reach:]
                    for i in rows:
                        for j in columns:
                            source = COLUMN[(kind, i - dr * height, j - dc * breadth)]
                            cells.append((kind, i, j, source))
                message.append(cells + [None] * (-len(cells) % 8))
            plan.append(message)
            starts.append(at)
            at += len(message[0]) + len(message[1])
        for start, message in zip(starts[first:], plan[first:]):
            for n, cell in enumerate(message[0] + message[1]):
                if cell:
                    COLUMN[cell[:3]] = start + n
    return plan, starts, at


PLAN, MSG_AT, KNOWN = message_plan()
MSG_ROWS = [end - start for start, end in zip(MSG_AT, MSG_AT[1:] + [KNOWN])]
MSG_CUT = [len(message[0]) for message in PLAN]
SIDE_END = MSG_AT[2]
SEND_SIDE = np.zeros((SIDE_END - LOC, LOC), np.float32)
SEND_ENDS = np.zeros((KNOWN - SIDE_END, SIDE_END), np.float32)
for n_, message_ in enumerate(PLAN):
    for m_, cell_ in enumerate(message_[0] + message_[1]):
        if cell_ and n_ < 2:
            SEND_SIDE[MSG_AT[n_] - LOC + m_, cell_[3]] = 1.0
        elif cell_:
            SEND_ENDS[MSG_AT[n_] - SIDE_END + m_, cell_[3]] = 1.0

STACKED = {}
STACK_ROWS = []
for part_ in (0, 1):
    at_ = G1 + G2
    for kind_, (height_, breadth_, _) in REACH.items():
        if kind_[0] == "db"[part_]:
            for i_ in range(height_):
                for j_ in range(breadth_):
                    STACKED[(kind_, i_, j_)] = local_row(kind_, i_, j_) - part_ * (G1 + G2)
    for message_ in PLAN:
        for m_, cell_ in enumerate(message_[part_]):
            if cell_:
                STACKED[cell_[:3]] = at_ + m_
        at_ += len(message_[part_])
    STACK_ROWS.append(at_)

INNER = G1 + G2
QROW = {}
for i_ in range(H1):
    for j_ in range(W1):
        QROW[(1, i_, j_)] = rho(i_, j_)
for i_ in range(H2):
    for j_ in range(W2):
        QROW[(2, i_, j_)] = G1 + i_ * W2 + j_
next_ = INNER
for level_, (height_, breadth_) in ((1, (H1, W1)), (2, (H2, W2))):
    for i_ in range(-1, height_ + 1):
        for j_ in range(-1, breadth_ + 1):
            if (level_, i_, j_) not in QROW:
                QROW[(level_, i_, j_)] = next_
                next_ += 1
QROWS = -(-next_ // 16) * 16

TAP_AT = np.full((QROWS, STACK_ROWS[0]), -1, np.int32)
PICK_BACK = np.zeros((QROWS, STACK_ROWS[1]), np.float32)
TAP_BACK = np.full((INNER, QROWS), -1, np.int32)
for (level_, i_, j_), q_ in QROW.items():
    PICK_BACK[q_, STACKED[("b%d" % level_, i_, j_)]] = 1.0
    for a_ in (-1, 0, 1):
        for b_ in (-1, 0, 1):
            tap_ = (level_ - 1) * 9 + (a_ + 1) * 3 + b_ + 1
            TAP_AT[q_, STACKED[("d%d" % level_, i_ + a_, j_ + b_)]] = tap_
            if q_ < INNER:
                TAP_BACK[q_, QROW[(level_, i_ - a_, j_ - b_)]] = tap_


def split(value):
    high = value.astype(BF)
    return high, (value - high.astype(F32)).astype(BF)


def mm(left, right):
    return jnp.dot(left, right, preferred_element_type=F32)


def rows_forward(parts, bands=(0, 1)):
    plus = [parts[0][k] + parts[1][k] for k in range(K)]
    minus = [parts[0][k] - parts[1][k] for k in range(K)]
    out = []
    for band in bands:
        outs = []
        for m in range(K):
            total = None
            for k in range(K):
                first, second = BANK[band, m, 0, k], BANK[band, m, 1, k]
                if first == 0.0:
                    continue
                term = (plus if first * second > 0 else minus)[k] * float(first)
                total = term if total is None else total + term
            outs.append(total)
        out.append(outs)
    return out


def rows_inverse(parts, bands=(0, 1)):
    out = [[None] * K, [None] * K]
    for k in range(K):
        same, other = None, None
        for band in bands:
            for m in range(K):
                first, second = BANK[band, m, 0, k], BANK[band, m, 1, k]
                if first == 0.0:
                    continue
                term = parts[band][m] * float(first)
                if first * second > 0:
                    same = term if same is None else same + term
                else:
                    other = term if other is None else other + term
        out[0][k] = same + other if other is not None else same
        out[1][k] = same - other if other is not None else same
    return out


def coarse_kernel(left_ref, wh_ref, wl_ref, field_ref, cot_ref, part_ref):
    count = K * G2
    found = []
    for source in (field_ref, cot_ref):
        total = None
        for k in range(K):
            term = mm(left_ref[k], source[:, k * QW : (k + 1) * QW])
            total = term if total is None else total + term
        found.append(total[: 4 * count] + total[4 * count :])
    state = None
    for j in range(4):
        piece = jnp.concatenate([part[j * count : (j + 1) * count] for part in found], axis=0)
        rows = slice(j * QW, (j + 1) * QW)
        term = times_filter(piece, wh_ref[rows], wl_ref[rows])
        state = term if state is None else state + term
    low_half = lax.broadcasted_iota(jnp.int32, (G2, 2 * CH), 1) < CH
    for m in range(K):
        for half in range(2):
            lanes = slice(half * 2 * CH, (half + 1) * 2 * CH)
            first = state[m * G2 : (m + 1) * G2, lanes]
            second = state[count + m * G2 : count + (m + 1) * G2, lanes]
            part_ref[m * K + 2 * half] = jnp.where(low_half, first, pltpu.roll(second, CH, 1))
            part_ref[m * K + 2 * half + 1] = jnp.where(low_half, pltpu.roll(first, CH, 1), second)


def analyze_kernel(stencil_ref, place_ref, field_ref, cot_ref, gather_ref, wh_ref, wl_ref, send_ref, tap_ref, tap_back_ref, places_ref, gains_ref, loc_ref, up_ref, down_ref, lead_ref, lead_back_ref, my_places_ref, my_gains_ref):
    gather = gather_ref[...]
    lefts = [[], []]
    for source in (field_ref, cot_ref):
        moved = mm(gather, source[...]).astype(BF)
        for a in range(2):
            for k in range(K):
                for b in range(2):
                    at = (a * 2 + b) * G1
                    lefts[b].append(moved[at : at + G1, k * QW : (k + 1) * QW])
    left = [jnp.concatenate(part, axis=0) for part in lefts]
    high = mm(left[0], wh_ref[: 2 * CH * 2]) + mm(left[1], wh_ref[2 * CH * 2 :])
    low = mm(left[0], wl_ref[: 2 * CH * 2]) + mm(left[1], wl_ref[2 * CH * 2 :])
    mixed = high + low
    lefts = [[], []]
    locs = []
    for n in range(2):
        parts = [[mixed[((n * 2 + a) * K + k) * G1 :][:G1] for k in range(K)] for a in range(2)]
        out = rows_forward(parts)
        detail = [out[0][m][:, QW:] for m in range(K)] + [out[1][m][:, :QW] for m in range(K)]
        detail += [out[1][m][:, QW:] for m in range(K)]
        locs.append(jnp.concatenate(detail, axis=1).astype(BF))
        for a in range(2):
            for k in range(K):
                for b in range(2):
                    at = (a * 2 + b) * G2
                    lefts[b].append(out[0][k][at : at + G2, :QW])
    mixed = None
    for b in range(2):
        high, low = split(jnp.concatenate(lefts[b], axis=0))
        rows = slice(b * QW, (b + 1) * QW)
        term = mm(high, wh_ref[rows]) + mm(low, wh_ref[rows]) + mm(high, wl_ref[rows])
        mixed = term if mixed is None else mixed + term
    for n in range(2):
        parts = [[mixed[((n * 2 + a) * K + k) * G2 :][:G2] for k in range(K)] for a in range(2)]
        out = rows_forward(parts)
        detail = [out[0][m][:, QW:] for m in range(K)] + [out[1][m][:, :QW] for m in range(K)]
        detail += [out[1][m][:, QW:] for m in range(K)]
        at = n * INNER
        loc_ref[at : at + G1, :] = locs[n]
        loc_ref[at + G1 : at + INNER, :] = jnp.concatenate(detail, axis=1).astype(BF)
    moved = mm(send_ref[...], loc_ref[...])
    up_ref[...] = moved[: MSG_ROWS[0]].astype(BF)
    down_ref[...] = moved[MSG_ROWS[0] :].astype(BF)
    up_ref.send()
    down_ref.send()
    loc_ref.send()
    taps = [stencil_ref[n] for n in range(18)]
    lead_ref[:QROWS], lead_ref[QROWS:] = split(tap_matrix(tap_ref[...], taps))
    lead_back_ref[:INNER], lead_back_ref[INNER:] = split(tap_matrix(tap_back_ref[...], taps))
    my_places_ref[...] = places_ref[...]
    gains = gains_ref[...]
    low_half = lax.broadcasted_iota(jnp.int32, gains.shape, 1) < CH
    even = (place_ref[0] % 2) == 0
    my_gains_ref[...] = jnp.where(low_half == even, gains, pltpu.roll(gains, CH, 1))


def stack(parts):
    return jnp.concatenate([part.astype(F32) for part in parts], axis=0).astype(BF)


def along_kernel(rows_ref, parts_ref, out_ref):
    out = mm3(rows_ref, parts_ref[...].reshape(-1, 2 * CH)).astype(BF)
    for n in range(out_ref.shape[0]):
        out_ref[n] = out


def ends_kernel(send_ref, loc_ref, up_ref, down_ref, left_ref, right_ref):
    known = jnp.concatenate([loc_ref[...], stack([up_ref[...], down_ref[...]])], axis=0)
    moved = mm(send_ref[...], known).astype(BF)
    left_ref[...] = moved[: MSG_ROWS[2]]
    right_ref[...] = moved[MSG_ROWS[2] :]


def modes_kernel(scale, across_ref, table_ref, rows_ref, gains_ref, parts_ref, out_ref):
    parts = parts_ref[...].reshape(-1, 2 * CH)
    modes = mm(across_ref[0], parts) + mm(across_ref[1], parts)
    wide = mm3(table_ref, gains_ref[...] * modes * scale)
    out_ref[...] = mm3(rows_ref, wide).reshape(out_ref.shape)


def mm3(left_ref, right):
    high, low = split(right)
    left_high = left_ref[0]
    return mm(left_high, high) + mm(left_ref[1], high) + mm(left_high, low)


def tap_matrix(at, taps):
    total = jnp.zeros(at.shape, F32)
    for n, tap in enumerate(taps):
        total = jnp.where(at == n, tap, total)
    return total


def detail_kernel(lead_ref, pick_ref, loc_ref, up_ref, down_ref, left_ref, right_ref, mix_ref, lead_back_ref, wh_ref, wl_ref, scatter_ref, out_ref, scratch):
    messages = [ref[...].astype(F32) for ref in (up_ref, down_ref, left_ref, right_ref)]
    details = [message[:cut] for message, cut in zip(messages, MSG_CUT)]
    others = [message[cut:] for message, cut in zip(messages, MSG_CUT)]
    details = jnp.concatenate([loc_ref[:INNER], stack(details)], axis=0)
    others = jnp.concatenate([loc_ref[INNER:], stack(others)], axis=0)
    lead, pick, lead_back = lead_ref[...], pick_ref[...], lead_back_ref[...]
    slope = math.sqrt(2.0 / math.pi)
    acts, derivatives, backs = [], [], []
    for band in range(3):
        lanes = slice(band * F, (band + 1) * F)
        found = mm(lead, details[:, lanes])
        pre = found[:QROWS] + found[QROWS:]
        square = pre * pre
        curve = jnp.tanh(slope * (pre + 0.044715 * (pre * square)))
        cdf = 0.5 * (1.0 + curve)
        acts.append((pre * cdf)[:INNER].astype(BF))
        derivatives.append(
            cdf + (0.5 * slope) * pre * (1.0 - curve * curve) * (1.0 + (3 * 0.044715) * square)
        )
        backs.append(mm(pick, others[:, lanes]).astype(BF))
    mix = mix_ref[...]
    mixed = mm(jnp.concatenate(acts, axis=0), mix)
    back = lax.dot_general(
        jnp.concatenate(backs, axis=0), mix, (((1,), (1,)), ((), ())), preferred_element_type=F32
    )
    for band in range(3):
        scratch[0, band] = mixed[band * INNER : (band + 1) * INNER]
        grad = (back[band * QROWS : (band + 1) * QROWS] * derivatives[band]).astype(BF)
        found = mm(lead_back, grad)
        scratch[1, band] = found[:INNER] + found[INNER:]
    found = synthesize(None, scratch, slice(G1, INNER), wh_ref, wl_ref)
    found = synthesize([place(out) for out in found], scratch, slice(0, G1), wh_ref, wl_ref)
    scatter = scatter_ref[...]
    for n in range(2):
        for k, block in enumerate(place(found[n])):
            out_ref[n, :, k * QW : (k + 1) * QW] = mm(scatter, block.astype(BF)).astype(BF)


def finish_kernel(wh_ref, wl_ref, left_ref, part_ref, coarse_ref, up_ref, down_ref):
    count = K * G2
    low_half = lax.broadcasted_iota(jnp.int32, (G2, 2 * CH), 1) < CH
    states = [[], []]
    for m in range(K):
        tiles = [[], []]
        for n in (2 * m, 2 * m + 1):
            first, second = coarse_ref[2 * n], coarse_ref[2 * n + 1]
            tiles[0].append(jnp.where(low_half, first, pltpu.roll(second, CH, 1)))
            tiles[1].append(jnp.where(low_half, pltpu.roll(first, CH, 1), second))
        for n in range(2):
            states[n].append(jnp.concatenate(tiles[n], axis=1))
    wide = times_filter(jnp.concatenate(states[0] + states[1], axis=0), wh_ref[...], wl_ref[...])
    for n, ref in enumerate((up_ref, down_ref)):
        rows = wide[n * count : (n + 1) * count]
        high, low = split(jnp.concatenate([rows[:, j * QW : (j + 1) * QW] for j in range(4)], axis=0))
        for k in range(K):
            lanes = slice(k * QW, (k + 1) * QW)
            left_high, left_low = left_ref[0, k], left_ref[1, k]
            found = mm(left_high, high) + mm(left_high, low) + mm(left_low, high)
            ref[:, lanes] = (part_ref[n, :, lanes] + found).astype(BF)
        ref.send()


def synthesize(states, scratch, rows, wh_ref, wl_ref):
    lefts = []
    for n in range(2):
        for band in range(2):
            for m in range(K):
                lanes = slice(m * QW, (m + 1) * QW)
                pair = [scratch[n, 1, rows, lanes], scratch[n, 2, rows, lanes]]
                if band == 0:
                    detail = scratch[n, 0, rows, lanes]
                    pair = [jnp.zeros_like(detail) if states is None else states[n][m], detail]
                lefts.append(jnp.concatenate(pair, axis=1))
    left = jnp.concatenate(lefts, axis=0).astype(BF)
    wide = mm(left, wh_ref[...]) + mm(left, wl_ref[...])
    count = rows.stop - rows.start
    out = []
    for n in range(2):
        parts = [[wide[((n * 2 + band) * K + m) * count :][:count] for m in range(K)] for band in range(2)]
        out.append(rows_inverse(parts))
    return out


def times_filter(left, high_filter, low_filter):
    high, low = split(left)
    return mm(high, high_filter) + mm(low, high_filter) + mm(high, low_filter)


def place(out):
    return [
        jnp.concatenate(
            [out[a][k][:, b * QW : (b + 1) * QW] for a in range(2) for b in range(2)], axis=0
        )
        for k in range(K)
    ]


def mode_tables(row_count, col_count):
    freqs = np.arange(MODES)
    angle = 2.0 * np.pi * np.outer(freqs, np.arange(row_count * H2)) / (row_count * H2)
    waves = np.stack([np.cos(angle), np.sin(angle)]).reshape(2, MODES, row_count, H2)
    rows = np.zeros((2, MODES, W2, row_count, G2))
    for i in range(H2):
        for j in range(W2):
            rows[:, :, j, :, i * W2 + j] = waves[:, :, :, i]
    rows = rows.reshape(2 * MODES * W2, row_count * G2)
    angle = 2.0 * np.pi * np.outer(freqs, np.arange(col_count * W2)) / (col_count * W2)
    cosine, sine = [part.reshape(MODES, col_count, W2) for part in (np.cos(angle), np.sin(angle))]
    places = np.zeros((col_count, 2, MODES, MODES, 2, MODES, W2))
    for u in range(MODES):
        for v in range(MODES):
            places[:, 0, u, v, 0, u] = cosine[v]
            places[:, 0, u, v, 1, u] = -sine[v]
            places[:, 1, u, v, 0, u] = sine[v]
            places[:, 1, u, v, 1, u] = cosine[v]
    places = places.reshape(col_count, 2 * MODES * MODES, 2 * MODES * W2)
    across = places.transpose(1, 0, 2).reshape(2 * MODES * MODES, -1)
    return [np.ascontiguousarray(part, np.float32) for part in (rows, rows.T, across, places.transpose(0, 2, 1))]


class Fetched:
    def __init__(self, source, scratch, sem):
        self.shape = scratch.shape
        self.ref = scratch
        self.copy = pltpu.make_async_copy(source, scratch, sem)
        self.copy.start()

    def arrived(self):
        if self.copy is not None:
            self.copy.wait()
            self.copy = None
        return self.ref

    def __getitem__(self, index):
        return self.arrived()[index]


class Returned:
    def __init__(self, target, scratch, sem):
        self.shape = scratch.shape
        self.ref = scratch
        self.copy = pltpu.make_async_copy(scratch, target, sem)
        self.started = False

    def __getitem__(self, index):
        return self.ref[index]

    def __setitem__(self, index, value):
        self.ref[index] = value

    def send(self):
        if not self.started:
            self.copy.start()
            self.started = True


def call(kernel, outs, ins, micros, smem=0, near=0, picks=None, near_out=False, scratch=(), limit=60):
    picks = picks or {}
    count, single = len(ins), not isinstance(outs, list)
    outs = [outs] if single else outs
    far = range(smem, count - near)
    blocks = [
        jax.eval_shape(lambda part, n=n: picks[n][0](part), ins[n]) if n in picks else ins[n] for n in far
    ]

    def wrapped(*refs):
        own = list(refs[:count])
        results = list(refs[count : count + len(outs)])
        rest = list(refs[count + len(outs) :])
        sems = rest.pop()
        for n, at in enumerate(far):
            source = picks[at][1](own[at], own[smem - 1]) if at in picks else own[at]
            own[at] = Fetched(source, rest.pop(0), sems.at[n])
        if not near_out:
            for n in range(len(outs)):
                results[n] = Returned(results[n], rest.pop(0), sems.at[len(far) + n])
        kernel(*own, *results, *rest)
        for operand in own:
            if isinstance(operand, Fetched):
                operand.arrived()
        if not near_out:
            for result in results:
                result.send()
            for result in results:
                result.copy.wait()

    where = [pltpu.SMEM] * smem + [pltpu.HBM] * len(far) + [pltpu.VMEM] * near
    inner = [pltpu.VMEM(block.shape, block.dtype) for block in blocks]
    if not near_out:
        inner += [pltpu.VMEM(out.shape, out.dtype) for out in outs]
    result = pl.pallas_call(
        wrapped,
        out_shape=outs,
        in_specs=[pl.BlockSpec(memory_space=space) for space in where],
        out_specs=[pl.BlockSpec(memory_space=pltpu.VMEM if near_out else pltpu.HBM) for _ in outs],
        scratch_shapes=inner + list(scratch) + [pltpu.SemaphoreType.DMA((len(far) + len(outs),))],
        compiler_params=pltpu.CompilerParams(vmem_limit_bytes=limit * 1024 * 1024),
        cost_estimate=pl.CostEstimate(
            flops=int(micros * 1.1e9), bytes_accessed=int(micros * 1e6), transcendentals=0
        ),
    )(*ins)
    return result[0] if single else result


def body(field, mix, stencil, spectral, cotangent):
    row_count, col_count = lax.axis_size("row"), lax.axis_size("col")
    wh, wl = [jnp.asarray(part) for part in halves(COL_FILTER)]
    wht, wlt = [jnp.asarray(np.ascontiguousarray(part.T)) for part in halves(COL_FILTER)]
    gather, scatter, send_side, send_ends, pick = [
        jnp.asarray(np.ascontiguousarray(part).astype(ml_dtypes.bfloat16))
        for part in (gather_table(), gather_table().T, SEND_SIDE, SEND_ENDS, PICK_BACK)
    ]
    rows, rows_back, across, places = [
        jnp.asarray(np.stack(halves(part), axis=part.ndim - 2))
        for part in mode_tables(row_count, col_count)
    ]
    place_here = jnp.stack([lax.axis_index("row"), lax.axis_index("col")])
    shape = jax.ShapeDtypeStruct

    def shift(message, dr, dc):
        axis, step = ("row", dr) if dr else ("col", dc)
        count = lax.axis_size(axis)
        return lax.ppermute(message, axis, [(n, (n - step) % count) for n in range(count)])

    def table(array):
        return jnp.asarray(np.ascontiguousarray(array))

    def high_low(array, axis):
        return table(np.concatenate(halves(array), axis=axis))

    coarse_filter = [table(part) for part in halves(COARSE_RIGHT)]
    coarse_back = [table(part.T) for part in halves(COARSE_RIGHT)]
    left_back = table(np.stack([part.transpose(0, 2, 1) for part in halves(COARSE_LEFT)]))
    field, cotangent = field.reshape(FI * FJ, F), cotangent.reshape(FI * FJ, F)
    part = call(
        coarse_kernel,
        shape((row_count, G2, 2 * CH), F32),
        (high_low(COARSE_LEFT, 1), *coarse_filter, field, cotangent),
        2,
        near_out=True,
    )
    part, field, cotangent = lax.optimization_barrier((part, field, cotangent))
    part = lax.all_to_all(part, "row", 0, 0, tiled=True)
    tile = 2 * CH
    loc, to_up, to_down, lead, lead_back, my_places, my_gains = call(
        analyze_kernel,
        [shape((LOC, 3 * F), BF)]
        + [shape((count, 3 * F), BF) for count in MSG_ROWS[:2]]
        + [shape((2 * QROWS, STACK_ROWS[0]), BF), shape((2 * INNER, QROWS), BF)]
        + [shape(places.shape[1:], BF), shape((2 * MODES * MODES, tile), F32)],
        (stencil.reshape(-1), place_here, field, cotangent, gather, wh, wl, send_side,
         jnp.asarray(TAP_AT), jnp.asarray(TAP_BACK), places, spectral.reshape(-1, F)),
        4,
        smem=2,
        picks={
            10: (lambda array: array[0], lambda ref, place: ref.at[place[1]]),
            11: (
                lambda array: array[:, :tile],
                lambda ref, place: ref.at[:, pl.ds(pl.multiple_of((place[0] // 2) * tile, tile), tile)],
            ),
        },
    )
    part = call(
        along_kernel,
        shape((col_count, 4 * MODES, tile), BF),
        (rows, part),
        1,
        near=2,
        near_out=True,
        limit=8,
    )
    part, to_up, to_down = lax.optimization_barrier((part, to_up, to_down))
    part = lax.all_to_all(part, "col", 0, 0, tiled=True)
    up, down = shift(to_up, *SIDES[0]), shift(to_down, *SIDES[1])
    to_left, to_right = call(
        ends_kernel,
        [shape((count, 3 * F), BF) for count in MSG_ROWS[2:]],
        (send_ends, loc, up, down),
        0.01,
    )
    left, right = shift(to_left, *SIDES[2]), shift(to_right, *SIDES[3])
    part = call(
        functools.partial(modes_kernel, 1.0 / math.sqrt(row_count * H2 * col_count * W2)),
        shape((row_count, G2, tile), F32),
        (across, my_places, rows_back, my_gains, part),
        1,
        near=5,
        near_out=True,
        limit=8,
    )
    part, loc = lax.optimization_barrier((part, loc))
    part = lax.all_to_all(part, "row", 0, 0, tiled=True)
    details = call(
        detail_kernel,
        shape((2, FI * FJ, F), BF),
        (lead, pick, loc, up, down, left, right, mix, lead_back, wht, wlt, scatter),
        7,
        scratch=[pltpu.VMEM((2, 3, INNER, F), F32)],
    )
    layer_out, grad_field = call(
        finish_kernel,
        [shape((FI * FJ, F), BF)] * 2,
        (*coarse_back, left_back, details, part),
        3,
        near=1,
    )
    return layer_out.reshape(FI, FJ, F), grad_field.reshape(FI, FJ, F)


def solution(mesh):
    placed = (P("row", "col", None), P(), P(), P(), P("row", "col", None))
    return jax.shard_map(
        body,
        mesh=mesh,
        in_specs=placed,
        out_specs=(P("row", "col", None), P("row", "col", None)),
        check_vma=False,
    )
```

```python
import functools
import math

import jax
import jax.numpy as jnp
import ml_dtypes
import numpy as np
from jax import lax
from jax.experimental import pallas as pl
from jax.experimental.pallas import tpu as pltpu
from jax.sharding import PartitionSpec as P

CH = 64
K = 4
MODES = 8
F = 1024
BF = jnp.bfloat16
F32 = jnp.float32
QW = K * CH

FI, FJ = 24, 8
H1, W1 = 12, 4
H2, W2 = 6, 2
G1, G2 = 64, 16
SIDES = [(-1, 0), (1, 0), (0, -1), (0, 1)]


def shifted_legendre(order_count):
    length = order_count + 1
    polys = [np.zeros(length), np.zeros(length)]
    polys[0][0] = 1.0
    polys[1][0] = -1.0
    polys[1][1] = 2.0
    for degree in range(1, order_count):
        times_t = np.zeros(length)
        times_t[1:] = 2.0 * polys[degree][:-1]
        times_t = times_t - polys[degree]
        polys.append(((2.0 * degree + 1.0) * times_t - degree * polys[degree - 1]) / (degree + 1.0))
    return [np.sqrt(2.0 * degree + 1.0) * polys[degree] for degree in range(order_count)]


def integrate_product(first, second):
    total = 0.0
    for power_a in range(first.shape[0]):
        for power_b in range(second.shape[0]):
            total = total + first[power_a] * second[power_b] / (power_a + power_b + 1.0)
    return total


def two_scale(order_count):
    polys = shifted_legendre(order_count)
    length = polys[0].shape[0]
    left_half = np.zeros((order_count, order_count))
    right_half = np.zeros((order_count, order_count))
    for out_index in range(order_count):
        coeffs = polys[out_index]
        halved = np.array([coeffs[power] * 0.5**power for power in range(length)])
        moved = np.zeros(length)
        for power in range(length):
            for lower in range(power + 1):
                moved[lower] = moved[lower] + coeffs[power] * 0.5**power * math.comb(power, lower)
        for in_index in range(order_count):
            left_half[out_index, in_index] = integrate_product(halved, polys[in_index]) / np.sqrt(2.0)
            right_half[out_index, in_index] = integrate_product(moved, polys[in_index]) / np.sqrt(2.0)
    scaling_rows = np.concatenate([left_half, right_half], axis=1)
    vectors = [scaling_rows[out_index] for out_index in range(order_count)]
    wavelet_rows = []
    for out_index in range(order_count):
        vector = np.zeros(2 * order_count)
        vector[out_index] = 1.0
        vector[order_count + out_index] = -1.0
        for earlier in vectors:
            vector = vector - np.dot(earlier, vector) * earlier
        vector = vector / np.sqrt(np.dot(vector, vector))
        vectors.append(vector)
        wavelet_rows.append(vector)
    return np.stack([scaling_rows, np.stack(wavelet_rows)]).reshape(2, order_count, 2, order_count)


BANK = two_scale(K)
BANK[np.abs(BANK) < 1e-12] = 0.0


def halves(array):
    high = np.asarray(array, np.float32).astype(ml_dtypes.bfloat16)
    low = (np.asarray(array, np.float64) - high.astype(np.float64)).astype(ml_dtypes.bfloat16)
    return high, low


COL_FILTER = np.kron(BANK.transpose(2, 3, 0, 1).reshape(2 * K, 2 * K), np.eye(CH))


def rho(i, j):
    return ((i % 2) * 2 + j % 2) * G2 + (i // 2) * W2 + j // 2


def local_row(kind, i, j):
    if kind == "d1":
        return rho(i, j)
    if kind == "d2":
        return G1 + i * W2 + j
    if kind == "b1":
        return G1 + G2 + rho(i, j)
    return 2 * G1 + G2 + i * W2 + j


LOC = 2 * (G1 + G2)
REACH = {"d1": (H1, W1, 2), "d2": (H2, W2, 2), "b1": (H1, W1, 1), "b2": (H2, W2, 1)}


TWICE = np.einsum("pbm,mak->pbak", BANK[0], BANK[0]).reshape(K, 4, K)
COARSE_LEFT = np.zeros((K, 4, K, G2, FI * FJ))
for i_ in range(FI):
    for j_ in range(FJ):
        COARSE_LEFT[:, j_ % 4, :, (i_ // 4) * W2 + j_ // 4, i_ * FJ + j_] = TWICE[:, i_ % 4, :].T
COARSE_LEFT = COARSE_LEFT.reshape(K, 4 * K * G2, FI * FJ)
COARSE_RIGHT = np.kron(TWICE.transpose(1, 2, 0).reshape(4 * K, K), np.eye(CH))
SUB = 32
TILE = 128


def gather_table():
    table = np.zeros((4 * G1, FI * FJ), np.float32)
    for i in range(FI):
        for j in range(FJ):
            table[((i % 2) * 2 + j % 2) * G1 + rho(i // 2, j // 2), i * FJ + j] = 1.0
    return table


COLUMN = {}
for kind_, (height_, breadth_, _) in REACH.items():
    for i_ in range(height_):
        for j_ in range(breadth_):
            COLUMN[(kind_, i_, j_)] = local_row(kind_, i_, j_)


def message_plan():
    at, plan, starts = LOC, [], []
    for first in (0, 2):
        for dr, dc in SIDES[first : first + 2]:
            message = []
            for part in ("d", "b"):
                cells = []
                for kind, (height, breadth, reach) in REACH.items():
                    if kind[0] != part:
                        continue
                    rows, columns = range(-reach, height + reach), range(-reach, breadth + reach)
                    if dr:
                        rows = rows[:reach] if dr < 0 else rows[-reach:]
                        columns = columns[reach:-reach]
                    else:
                        columns = columns[:reach] if dc < 0 else columns[-reach:]
                    for i in rows:
                        for j in columns:
                            source = COLUMN[(kind, i - dr * height, j - dc * breadth)]
                            cells.append((kind, i, j, source))
                message.append(cells + [None] * (-len(cells) % 8))
            plan.append(message)
            starts.append(at)
            at += len(message[0]) + len(message[1])
        for start, message in zip(starts[first:], plan[first:]):
            for n, cell in enumerate(message[0] + message[1]):
                if cell:
                    COLUMN[cell[:3]] = start + n
    return plan, starts, at


PLAN, MSG_AT, KNOWN = message_plan()
MSG_ROWS = [end - start for start, end in zip(MSG_AT, MSG_AT[1:] + [KNOWN])]
MSG_CUT = [len(message[0]) for message in PLAN]
SIDE_END = MSG_AT[2]
SEND_SIDE = np.zeros((SIDE_END - LOC, LOC), np.float32)
SEND_ENDS = np.zeros((KNOWN - SIDE_END, SIDE_END), np.float32)
for n_, message_ in enumerate(PLAN):
    for m_, cell_ in enumerate(message_[0] + message_[1]):
        if cell_ and n_ < 2:
            SEND_SIDE[MSG_AT[n_] - LOC + m_, cell_[3]] = 1.0
        elif cell_:
            SEND_ENDS[MSG_AT[n_] - SIDE_END + m_, cell_[3]] = 1.0

STACKED = {}
STACK_ROWS = []
for part_ in (0, 1):
    at_ = G1 + G2
    for kind_, (height_, breadth_, _) in REACH.items():
        if kind_[0] == "db"[part_]:
            for i_ in range(height_):
                for j_ in range(breadth_):
                    STACKED[(kind_, i_, j_)] = local_row(kind_, i_, j_) - part_ * (G1 + G2)
    for message_ in PLAN:
        for m_, cell_ in enumerate(message_[part_]):
            if cell_:
                STACKED[cell_[:3]] = at_ + m_
        at_ += len(message_[part_])
    STACK_ROWS.append(at_)

INNER = G1 + G2
QROW = {}
for i_ in range(H1):
    for j_ in range(W1):
        QROW[(1, i_, j_)] = rho(i_, j_)
for i_ in range(H2):
    for j_ in range(W2):
        QROW[(2, i_, j_)] = G1 + i_ * W2 + j_
next_ = INNER
for level_, (height_, breadth_) in ((1, (H1, W1)), (2, (H2, W2))):
    for i_ in range(-1, height_ + 1):
        for j_ in range(-1, breadth_ + 1):
            if (level_, i_, j_) not in QROW:
                QROW[(level_, i_, j_)] = next_
                next_ += 1
QROWS = -(-next_ // 16) * 16

TAP_AT = np.full((QROWS, STACK_ROWS[0]), -1, np.int32)
PICK_BACK = np.zeros((QROWS, STACK_ROWS[1]), np.float32)
TAP_BACK = np.full((INNER, QROWS), -1, np.int32)
for (level_, i_, j_), q_ in QROW.items():
    PICK_BACK[q_, STACKED[("b%d" % level_, i_, j_)]] = 1.0
    for a_ in (-1, 0, 1):
        for b_ in (-1, 0, 1):
            tap_ = (level_ - 1) * 9 + (a_ + 1) * 3 + b_ + 1
            TAP_AT[q_, STACKED[("d%d" % level_, i_ + a_, j_ + b_)]] = tap_
            if q_ < INNER:
                TAP_BACK[q_, QROW[(level_, i_ - a_, j_ - b_)]] = tap_


def split(value):
    high = value.astype(BF)
    return high, (value - high.astype(F32)).astype(BF)


def mm(left, right):
    return jnp.dot(left, right, preferred_element_type=F32)


def rows_forward(parts, bands=(0, 1)):
    plus = [parts[0][k] + parts[1][k] for k in range(K)]
    minus = [parts[0][k] - parts[1][k] for k in range(K)]
    out = []
    for band in bands:
        outs = []
        for m in range(K):
            total = None
            for k in range(K):
                first, second = BANK[band, m, 0, k], BANK[band, m, 1, k]
                if first == 0.0:
                    continue
                term = (plus if first * second > 0 else minus)[k] * float(first)
                total = term if total is None else total + term
            outs.append(total)
        out.append(outs)
    return out


def rows_inverse(parts, bands=(0, 1)):
    out = [[None] * K, [None] * K]
    for k in range(K):
        same, other = None, None
        for band in bands:
            for m in range(K):
                first, second = BANK[band, m, 0, k], BANK[band, m, 1, k]
                if first == 0.0:
                    continue
                term = parts[band][m] * float(first)
                if first * second > 0:
                    same = term if same is None else same + term
                else:
                    other = term if other is None else other + term
        out[0][k] = same + other if other is not None else same
        out[1][k] = same - other if other is not None else same
    return out


def quarter(index):
    return lax.broadcasted_iota(jnp.int32, (8, TILE), 1) // SUB == index


def pack_channels(first, second, out_ref):
    for n in range(F // TILE):
        lanes = slice(n * TILE, (n + 1) * TILE)
        sources = [first[:8, lanes], second[:8, lanes], first[8:, lanes], second[8:, lanes]]
        for s in range(TILE // SUB):
            total = None
            for t, source in enumerate(sources):
                moved = source if s == t else pltpu.roll(source, (t - s) % 4 * SUB, 1)
                total = moved if total is None else jnp.where(quarter(t), moved, total)
            out_ref[n * 4 + s] = total


def unpack_channels(ref):
    out = [[], []]
    for n in range(F // TILE):
        sources = [ref[n * 4 + s] for s in range(TILE // SUB)]
        found = []
        for t in range(4):
            total = None
            for s, source in enumerate(sources):
                moved = source if s == t else pltpu.roll(source, (s - t) % 4 * SUB, 1)
                total = moved if total is None else jnp.where(quarter(s), moved, total)
            found.append(total)
        out[0].append(jnp.concatenate([found[0], found[2]], axis=0))
        out[1].append(jnp.concatenate([found[1], found[3]], axis=0))
    return out


def analyze_kernel(field_ref, cot_ref, gather_ref, wh_ref, wl_ref, send_ref, loc_ref, up_ref, down_ref, part_ref):
    gather = gather_ref[...]
    lefts = [[], []]
    for source in (field_ref, cot_ref):
        moved = mm(gather, source[...]).astype(BF)
        for a in range(2):
            for k in range(K):
                for b in range(2):
                    at = (a * 2 + b) * G1
                    lefts[b].append(moved[at : at + G1, k * QW : (k + 1) * QW])
    left = [jnp.concatenate(part, axis=0) for part in lefts]
    high = mm(left[0], wh_ref[: 2 * CH * 2]) + mm(left[1], wh_ref[2 * CH * 2 :])
    low = mm(left[0], wl_ref[: 2 * CH * 2]) + mm(left[1], wl_ref[2 * CH * 2 :])
    mixed = high + low
    lefts = [[], []]
    locs = []
    for n in range(2):
        parts = [[mixed[((n * 2 + a) * K + k) * G1 :][:G1] for k in range(K)] for a in range(2)]
        out = rows_forward(parts)
        detail = [out[0][m][:, QW:] for m in range(K)] + [out[1][m][:, :QW] for m in range(K)]
        detail += [out[1][m][:, QW:] for m in range(K)]
        locs.append(jnp.concatenate(detail, axis=1).astype(BF))
        for a in range(2):
            for k in range(K):
                for b in range(2):
                    at = (a * 2 + b) * G2
                    lefts[b].append(out[0][k][at : at + G2, :QW])
    mixed = None
    for b in range(2):
        high, low = split(jnp.concatenate(lefts[b], axis=0))
        rows = slice(b * QW, (b + 1) * QW)
        term = mm(high, wh_ref[rows]) + mm(low, wh_ref[rows]) + mm(high, wl_ref[rows])
        mixed = term if mixed is None else mixed + term
    coarse = []
    for n in range(2):
        parts = [[mixed[((n * 2 + a) * K + k) * G2 :][:G2] for k in range(K)] for a in range(2)]
        out = rows_forward(parts)
        detail = [out[0][m][:, QW:] for m in range(K)] + [out[1][m][:, :QW] for m in range(K)]
        detail += [out[1][m][:, QW:] for m in range(K)]
        at = n * INNER
        loc_ref[at : at + G1, :] = locs[n]
        loc_ref[at + G1 : at + INNER, :] = jnp.concatenate(detail, axis=1).astype(BF)
        coarse.append(jnp.concatenate([out[0][m][:, :QW] for m in range(K)], axis=1))
    pack_channels(*coarse, part_ref)
    part_ref.send()
    loc_ref.send()
    moved = mm(send_ref[...], loc_ref[...])
    up_ref[...] = moved[: MSG_ROWS[0]].astype(BF)
    down_ref[...] = moved[MSG_ROWS[0] :].astype(BF)


def stack(parts):
    return jnp.concatenate([part.astype(F32) for part in parts], axis=0).astype(BF)


def along_kernel(rows_ref, parts_ref, out_ref):
    high, low = split(parts_ref[...].reshape(-1, TILE))

    def times(n):
        left_high = rows_ref[n, 0]
        return mm(left_high, high) + mm(rows_ref[n, 1], high) + mm(left_high, low)

    near = lax.broadcasted_iota(jnp.int32, (4 * MODES, TILE), 1) < TILE // 2
    first = times(0) + pltpu.roll(times(1), TILE // 2, 1)
    second = pltpu.roll(times(2), TILE // 2, 1) + times(3)
    out = jnp.where(near, first, second).astype(BF)
    for n in range(out_ref.shape[0]):
        out_ref[n] = out


def ends_kernel(stencil_ref, send_ref, loc_ref, up_ref, down_ref, tap_ref, tap_back_ref, places_ref, gains_ref, left_ref, right_ref, lead_ref, lead_back_ref, my_places_ref, my_gains_ref):
    known = jnp.concatenate([loc_ref[...], stack([up_ref[...], down_ref[...]])], axis=0)
    moved = mm(send_ref[...], known).astype(BF)
    left_ref[...] = moved[: MSG_ROWS[2]]
    left_ref.send()
    right_ref[...] = moved[MSG_ROWS[2] :]
    right_ref.send()
    taps = [stencil_ref[n // 9, n // 3 % 3, n % 3] for n in range(18)]
    lead_ref[:QROWS], lead_ref[QROWS:] = split(tap_matrix(tap_ref[...], taps))
    lead_back_ref[:INNER], lead_back_ref[INNER:] = split(tap_matrix(tap_back_ref[...], taps))
    my_places_ref[...] = places_ref[...]
    gains = gains_ref[...]
    own = (lax.axis_index("row") * 2 + lax.axis_index("col") % 2) % 4
    group = lax.broadcasted_iota(jnp.int32, gains.shape, 1) // SUB
    total = jnp.zeros_like(gains)
    for s in range(4):
        for t in range(2):
            moved = pltpu.roll(gains, (t - s) % 4 * SUB, 1) if s != t else gains
            total = jnp.where((group == t) & (own == s), moved, total)
    my_gains_ref[...] = total


def modes_kernel(scale, across_ref, table_ref, rows_ref, gains_ref, parts_ref, out_ref):
    parts = parts_ref[...].reshape(-1, TILE)
    half = TILE // 2
    modes = mm(across_ref[0, 0], parts) + mm(across_ref[0, 1], parts)
    modes = modes + pltpu.roll(mm(across_ref[1, 0], parts) + mm(across_ref[1, 1], parts), half, 1)
    coeffs = gains_ref[...] * modes * scale
    near = lax.broadcasted_iota(jnp.int32, (4 * MODES, TILE), 1) < half
    wide = jnp.where(
        near, mm3(table_ref.at[0], coeffs), pltpu.roll(mm3(table_ref.at[1], coeffs), half, 1)
    )
    first, second = mm3(rows_ref.at[0], wide), mm3(rows_ref.at[1], wide)
    near = lax.broadcasted_iota(jnp.int32, first.shape, 1) < half
    shape = (out_ref.shape[0], 8, TILE)
    out_ref[:, 0] = jnp.where(near, first, pltpu.roll(second, half, 1)).reshape(shape)
    out_ref[:, 1] = jnp.where(near, pltpu.roll(first, half, 1), second).reshape(shape)


def mm3(left_ref, right):
    high, low = split(right)
    left_high = left_ref[0]
    return mm(left_high, high) + mm(left_ref[1], high) + mm(left_high, low)


def tap_matrix(at, taps):
    total = jnp.zeros(at.shape, F32)
    for n, tap in enumerate(taps):
        total = jnp.where(at == n, tap, total)
    return total


def detail_kernel(lead_ref, pick_ref, loc_ref, up_ref, down_ref, left_ref, right_ref, mix_ref, lead_back_ref, wh_ref, wl_ref, scatter_ref, out_ref, scratch):
    messages = [ref[...].astype(F32) for ref in (up_ref, down_ref, left_ref, right_ref)]
    details = [message[:cut] for message, cut in zip(messages, MSG_CUT)]
    others = [message[cut:] for message, cut in zip(messages, MSG_CUT)]
    details = jnp.concatenate([loc_ref[:INNER], stack(details)], axis=0)
    others = jnp.concatenate([loc_ref[INNER:], stack(others)], axis=0)
    lead, pick, lead_back = lead_ref[...], pick_ref[...], lead_back_ref[...]
    slope = math.sqrt(2.0 / math.pi)
    acts, derivatives, backs = [], [], []
    for band in range(3):
        lanes = slice(band * F, (band + 1) * F)
        found = mm(lead, details[:, lanes])
        pre = found[:QROWS] + found[QROWS:]
        square = pre * pre
        curve = jnp.tanh(slope * (pre + 0.044715 * (pre * square)))
        cdf = 0.5 * (1.0 + curve)
        acts.append((pre * cdf)[:INNER].astype(BF))
        derivatives.append(
            cdf + (0.5 * slope) * pre * (1.0 - curve * curve) * (1.0 + (3 * 0.044715) * square)
        )
        backs.append(mm(pick, others[:, lanes]).astype(BF))
    mix = mix_ref[...]
    mixed = mm(jnp.concatenate(acts, axis=0), mix)
    back = lax.dot_general(
        jnp.concatenate(backs, axis=0), mix, (((1,), (1,)), ((), ())), preferred_element_type=F32
    )
    for band in range(3):
        scratch[0, band] = mixed[band * INNER : (band + 1) * INNER].astype(BF)
        grad = (back[band * QROWS : (band + 1) * QROWS] * derivatives[band]).astype(BF)
        found = mm(lead_back, grad)
        scratch[1, band] = (found[:INNER] + found[INNER:]).astype(BF)
    found = synthesize(None, scratch, slice(G1, INNER), wh_ref, wl_ref)
    found = synthesize([[part.astype(BF) for part in place(out)] for out in found], scratch, slice(0, G1), wh_ref, wl_ref)
    scatter = scatter_ref[...]
    for n in range(2):
        for k, block in enumerate(place(found[n])):
            out_ref[n, :, k * QW : (k + 1) * QW] = mm(scatter, block.astype(BF)).astype(BF)


def finish_kernel(wh_ref, wl_ref, left_ref, part_ref, coarse_ref, up_ref, down_ref):
    count = K * G2
    tiles = unpack_channels(coarse_ref)
    states = [
        [jnp.concatenate(own[2 * m : 2 * m + 2], axis=1) for m in range(K)] for own in tiles
    ]
    wide = times_filter(jnp.concatenate(states[0] + states[1], axis=0), wh_ref[...], wl_ref[...])
    for n, ref in enumerate((up_ref, down_ref)):
        rows = wide[n * count : (n + 1) * count]
        high, low = split(jnp.concatenate([rows[:, j * QW : (j + 1) * QW] for j in range(4)], axis=0))
        for k in range(K):
            lanes = slice(k * QW, (k + 1) * QW)
            left_high, left_low = left_ref[0, k], left_ref[1, k]
            found = mm(left_high, high) + mm(left_high, low) + mm(left_low, high)
            ref[:, lanes] = (part_ref[n, :, lanes] + found).astype(BF)
        ref.send()


def synthesize(states, scratch, rows, wh_ref, wl_ref):
    lefts = []
    for n in range(2):
        for band in range(2):
            for m in range(K):
                lanes = slice(m * QW, (m + 1) * QW)
                pair = [scratch[n, 1, rows, lanes], scratch[n, 2, rows, lanes]]
                if band == 0:
                    detail = scratch[n, 0, rows, lanes]
                    pair = [jnp.zeros_like(detail) if states is None else states[n][m], detail]
                lefts.append(jnp.concatenate(pair, axis=1))
    left = jnp.concatenate(lefts, axis=0)
    wide = mm(left, wh_ref[...]) + mm(left, wl_ref[...])
    count = rows.stop - rows.start
    out = []
    for n in range(2):
        parts = [[wide[((n * 2 + band) * K + m) * count :][:count] for m in range(K)] for band in range(2)]
        out.append(rows_inverse(parts))
    return out


def times_filter(left, high_filter, low_filter):
    high, low = split(left)
    return mm(high, high_filter) + mm(low, high_filter) + mm(high, low_filter)


def place(out):
    return [
        jnp.concatenate(
            [out[a][k][:, b * QW : (b + 1) * QW] for a in range(2) for b in range(2)], axis=0
        )
        for k in range(K)
    ]


def mode_tables(row_count, chip_count):
    freqs = np.arange(MODES)
    angle = 2.0 * np.pi * np.outer(freqs, np.arange(row_count * H2)) / (row_count * H2)
    waves = np.stack([np.cos(angle), np.sin(angle)]).reshape(2, MODES, row_count, H2)
    rows = np.zeros((2, MODES, W2, row_count, G2))
    for i in range(H2):
        for j in range(W2):
            rows[:, :, j, :, i * W2 + j] = waves[:, :, :, i]
    rows = rows.reshape(2 * MODES * W2, row_count, 2, 8)
    back = rows.transpose(2, 1, 3, 0).reshape(2, row_count * 8, -1)
    along = np.zeros((2, 2, 2 * MODES * W2, row_count, 2, 8))
    for core in range(2):
        for half in range(2):
            along[core, half, :, :, core] = rows[:, :, half]
    along = along.reshape(4, 2 * MODES * W2, -1)
    angle = 2.0 * np.pi * np.outer(freqs, np.arange(chip_count * 2 * W2)) / (chip_count * 2 * W2)
    cosine, sine = [part.reshape(MODES, chip_count, 2, W2) for part in (np.cos(angle), np.sin(angle))]
    places = np.zeros((chip_count, 2, 2, MODES, MODES, 2, MODES, W2))
    for u in range(MODES):
        for v in range(MODES):
            places[:, :, 0, u, v, 0, u] = cosine[v]
            places[:, :, 0, u, v, 1, u] = -sine[v]
            places[:, :, 1, u, v, 0, u] = sine[v]
            places[:, :, 1, u, v, 1, u] = cosine[v]
    places = places.reshape(chip_count, 2, 2 * MODES * MODES, 2 * MODES * W2)
    across = places.transpose(1, 2, 0, 3).reshape(2, 2 * MODES * MODES, -1)
    places = places.transpose(0, 1, 3, 2)
    return [jnp.asarray(np.stack(halves(part), axis=part.ndim - 2)) for part in (along, back, across, places)]


class Fetched:
    def __init__(self, source, scratch, sem):
        self.shape = scratch.shape
        self.ref = scratch
        self.copy = pltpu.make_async_copy(source, scratch, sem)
        self.copy.start()

    def arrived(self):
        if self.copy is not None:
            self.copy.wait()
            self.copy = None
        return self.ref

    def __getitem__(self, index):
        return self.arrived()[index]


class Returned:
    def __init__(self, target, scratch, sem):
        self.shape = scratch.shape
        self.ref = scratch
        self.copy = pltpu.make_async_copy(scratch, target, sem)
        self.started = False

    def __getitem__(self, index):
        return self.ref[index]

    def __setitem__(self, index, value):
        self.ref[index] = value

    def send(self):
        if not self.started:
            self.copy.start()
            self.started = True


def call(kernel, outs, ins, micros, smem=0, near=0, picks=None, near_out=False, scratch=(), limit=60):
    picks = picks or {}
    count, single = len(ins), not isinstance(outs, list)
    outs = [outs] if single else outs
    far = range(smem, count - near)
    blocks = [
        jax.eval_shape(lambda part, n=n: picks[n][0](part), ins[n]) if n in picks else ins[n] for n in far
    ]

    def wrapped(*refs):
        own = list(refs[:count])
        results = list(refs[count : count + len(outs)])
        rest = list(refs[count + len(outs) :])
        sems = rest.pop()
        for n, at in enumerate(far):
            source = picks[at][1](own[at]) if at in picks else own[at]
            own[at] = Fetched(source, rest.pop(0), sems.at[n])
        if not near_out:
            for n in range(len(outs)):
                results[n] = Returned(results[n], rest.pop(0), sems.at[len(far) + n])
        kernel(*own, *results, *rest)
        for operand in own:
            if isinstance(operand, Fetched):
                operand.arrived()
        if not near_out:
            for result in results:
                result.send()
            for result in results:
                result.copy.wait()

    where = [pltpu.SMEM] * smem + [pltpu.HBM] * len(far) + [pltpu.VMEM] * near
    inner = [pltpu.VMEM(block.shape, block.dtype) for block in blocks]
    if not near_out:
        inner += [pltpu.VMEM(out.shape, out.dtype) for out in outs]
    result = pl.pallas_call(
        wrapped,
        out_shape=outs,
        in_specs=[pl.BlockSpec(memory_space=space) for space in where],
        out_specs=[pl.BlockSpec(memory_space=pltpu.VMEM if near_out else pltpu.HBM) for _ in outs],
        scratch_shapes=inner + list(scratch) + [pltpu.SemaphoreType.DMA((len(far) + len(outs),))],
        compiler_params=pltpu.CompilerParams(vmem_limit_bytes=limit * 1024 * 1024),
        cost_estimate=pl.CostEstimate(
            flops=int(micros * 1.1e9), bytes_accessed=int(micros * 1e6), transcendentals=0
        ),
    )(*ins)
    return result[0] if single else result


def body(field, mix, stencil, spectral, cotangent):
    row_count, col_count = lax.axis_size("row"), lax.axis_size("col")
    wh, wl = [jnp.asarray(part) for part in halves(COL_FILTER)]
    wht, wlt = [jnp.asarray(np.ascontiguousarray(part.T)) for part in halves(COL_FILTER)]
    gather, scatter, send_side, send_ends, pick = [
        jnp.asarray(np.ascontiguousarray(part).astype(ml_dtypes.bfloat16))
        for part in (gather_table(), gather_table().T, SEND_SIDE, SEND_ENDS, PICK_BACK)
    ]
    chip_count = col_count // 2
    along, back, across, places = mode_tables(row_count, chip_count)
    shape = jax.ShapeDtypeStruct

    def table(array):
        return jnp.asarray(np.ascontiguousarray(array))

    def shift(message, dr, dc):
        axis, step = ("row", dr) if dr else ("col", dc)
        count = lax.axis_size(axis)
        return lax.ppermute(message, axis, [(n, (n - step) % count) for n in range(count)])

    coarse_back = [table(part.T) for part in halves(COARSE_RIGHT)]
    left_back = table(np.stack([part.transpose(0, 2, 1) for part in halves(COARSE_LEFT)]))
    plane = [
        [r * col_count + 2 * z + core for r in range(row_count) for core in range(2)]
        for z in range(chip_count)
    ]
    chips = [[2 * z + core for z in range(chip_count)] for core in range(2)]

    def over_plane(pieces):
        return lax.all_to_all(pieces, ("row", "col"), 0, 0, tiled=True, axis_index_groups=plane)

    loc, to_up, to_down, part = call(
        analyze_kernel,
        [shape((LOC, 3 * F), BF)]
        + [shape((count, 3 * F), BF) for count in MSG_ROWS[:2]]
        + [shape((2 * row_count, 8, TILE), F32)],
        (field.reshape(FI * FJ, F), cotangent.reshape(FI * FJ, F), gather, wh, wl, send_side),
        4,
    )
    part = over_plane(part)
    up, down = shift(to_up, *SIDES[0]), shift(to_down, *SIDES[1])
    part = call(
        along_kernel,
        shape((chip_count, 4 * MODES, TILE), BF),
        (along, part),
        1,
        near=2,
        near_out=True,
        limit=8,
    )
    part, loc = lax.optimization_barrier((part, loc))
    part = lax.all_to_all(part, "col", 0, 0, tiled=True, axis_index_groups=chips)
    to_left, to_right, lead, lead_back, my_places, my_gains = call(
        ends_kernel,
        [shape((count, 3 * F), BF) for count in MSG_ROWS[2:]]
        + [shape((2 * QROWS, STACK_ROWS[0]), BF), shape((2 * INNER, QROWS), BF)]
        + [shape(places.shape[1:], BF), shape((2 * MODES * MODES, TILE), F32)],
        (stencil, send_ends, loc, up, down, jnp.asarray(TAP_AT), jnp.asarray(TAP_BACK), places,
         spectral.reshape(-1, F)),
        0.01,
        smem=1,
        picks={
            7: (lambda array: array[0], lambda ref: ref.at[lax.axis_index("col") // 2]),
            8: (
                lambda array: array[:, :TILE],
                lambda ref: ref.at[:, pl.ds(pl.multiple_of(lax.axis_index("row") // 2 * TILE, TILE), TILE)],
            ),
        },
    )
    left, right = shift(to_left, *SIDES[2]), shift(to_right, *SIDES[3])
    part = call(
        functools.partial(modes_kernel, 1.0 / math.sqrt(row_count * H2 * col_count * W2)),
        shape((row_count, 2, 8, TILE), F32),
        (across, my_places, back, my_gains, part),
        1,
        near=5,
        near_out=True,
        limit=8,
    )
    part, loc = lax.optimization_barrier((part, loc))
    part = over_plane(part.reshape(2 * row_count, 8, TILE))
    details = call(
        detail_kernel,
        shape((2, FI * FJ, F), BF),
        (lead, pick, loc, up, down, left, right, mix, lead_back, wht, wlt, scatter),
        7,
        scratch=[pltpu.VMEM((2, 3, INNER, F), BF)],
    )
    layer_out, grad_field = call(
        finish_kernel,
        [shape((FI * FJ, F), BF)] * 2,
        (*coarse_back, left_back, details, part),
        3,
        near=1,
    )
    return layer_out.reshape(FI, FJ, F), grad_field.reshape(FI, FJ, F)


def solution(mesh):
    placed = (P("row", "col", None), P(), P(), P(), P("row", "col", None))
    return jax.shard_map(
        body,
        mesh=mesh,
        in_specs=placed,
        out_specs=(P("row", "col", None), P("row", "col", None)),
        check_vma=False,
    )
```

```python
import functools
import math

import jax
import jax.numpy as jnp
import ml_dtypes
import numpy as np
from jax import lax
from jax.experimental import pallas as pl
from jax.experimental.pallas import tpu as pltpu
from jax.sharding import PartitionSpec as P

CH = 64
K = 4
MODES = 8
F = 1024
BF = jnp.bfloat16
F32 = jnp.float32
QW = K * CH

FI, FJ = 24, 8
H1, W1 = 12, 4
H2, W2 = 6, 2
G1, G2 = 64, 16
SIDES = [(-1, 0), (1, 0), (0, -1), (0, 1)]


def shifted_legendre(order_count):
    length = order_count + 1
    polys = [np.zeros(length), np.zeros(length)]
    polys[0][0] = 1.0
    polys[1][0] = -1.0
    polys[1][1] = 2.0
    for degree in range(1, order_count):
        times_t = np.zeros(length)
        times_t[1:] = 2.0 * polys[degree][:-1]
        times_t = times_t - polys[degree]
        polys.append(((2.0 * degree + 1.0) * times_t - degree * polys[degree - 1]) / (degree + 1.0))
    return [np.sqrt(2.0 * degree + 1.0) * polys[degree] for degree in range(order_count)]


def integrate_product(first, second):
    total = 0.0
    for power_a in range(first.shape[0]):
        for power_b in range(second.shape[0]):
            total = total + first[power_a] * second[power_b] / (power_a + power_b + 1.0)
    return total


def two_scale(order_count):
    polys = shifted_legendre(order_count)
    length = polys[0].shape[0]
    left_half = np.zeros((order_count, order_count))
    right_half = np.zeros((order_count, order_count))
    for out_index in range(order_count):
        coeffs = polys[out_index]
        halved = np.array([coeffs[power] * 0.5**power for power in range(length)])
        moved = np.zeros(length)
        for power in range(length):
            for lower in range(power + 1):
                moved[lower] = moved[lower] + coeffs[power] * 0.5**power * math.comb(power, lower)
        for in_index in range(order_count):
            left_half[out_index, in_index] = integrate_product(halved, polys[in_index]) / np.sqrt(2.0)
            right_half[out_index, in_index] = integrate_product(moved, polys[in_index]) / np.sqrt(2.0)
    scaling_rows = np.concatenate([left_half, right_half], axis=1)
    vectors = [scaling_rows[out_index] for out_index in range(order_count)]
    wavelet_rows = []
    for out_index in range(order_count):
        vector = np.zeros(2 * order_count)
        vector[out_index] = 1.0
        vector[order_count + out_index] = -1.0
        for earlier in vectors:
            vector = vector - np.dot(earlier, vector) * earlier
        vector = vector / np.sqrt(np.dot(vector, vector))
        vectors.append(vector)
        wavelet_rows.append(vector)
    return np.stack([scaling_rows, np.stack(wavelet_rows)]).reshape(2, order_count, 2, order_count)


BANK = two_scale(K)
BANK[np.abs(BANK) < 1e-12] = 0.0


def halves(array):
    high = np.asarray(array, np.float32).astype(ml_dtypes.bfloat16)
    low = (np.asarray(array, np.float64) - high.astype(np.float64)).astype(ml_dtypes.bfloat16)
    return high, low


COL_FILTER = np.kron(BANK.transpose(2, 3, 0, 1).reshape(2 * K, 2 * K), np.eye(CH))


def rho(i, j):
    return ((i % 2) * 2 + j % 2) * G2 + (i // 2) * W2 + j // 2


def local_row(kind, i, j):
    if kind == "d1":
        return rho(i, j)
    if kind == "d2":
        return G1 + i * W2 + j
    if kind == "b1":
        return G1 + G2 + rho(i, j)
    return 2 * G1 + G2 + i * W2 + j


LOC = 2 * (G1 + G2)
REACH = {"d1": (H1, W1, 2), "d2": (H2, W2, 2), "b1": (H1, W1, 1), "b2": (H2, W2, 1)}


TWICE = np.einsum("pbm,mak->pbak", BANK[0], BANK[0]).reshape(K, 4, K)
COARSE_LEFT = np.zeros((K, 4, K, G2, FI * FJ))
for i_ in range(FI):
    for j_ in range(FJ):
        COARSE_LEFT[:, j_ % 4, :, (i_ // 4) * W2 + j_ // 4, i_ * FJ + j_] = TWICE[:, i_ % 4, :].T
COARSE_LEFT = COARSE_LEFT.reshape(K, 4 * K * G2, FI * FJ)
COARSE_RIGHT = np.kron(TWICE.transpose(1, 2, 0).reshape(4 * K, K), np.eye(CH))
SUB = 32
TILE = 128


def gather_table():
    table = np.zeros((4 * G1, FI * FJ), np.float32)
    for i in range(FI):
        for j in range(FJ):
            table[((i % 2) * 2 + j % 2) * G1 + rho(i // 2, j // 2), i * FJ + j] = 1.0
    return table


COLUMN = {}
for kind_, (height_, breadth_, _) in REACH.items():
    for i_ in range(height_):
        for j_ in range(breadth_):
            COLUMN[(kind_, i_, j_)] = local_row(kind_, i_, j_)


def message_plan():
    at, plan, starts = LOC, [], []
    for first in (0, 2):
        for dr, dc in SIDES[first : first + 2]:
            message = []
            for part in ("d", "b"):
                cells = []
                for kind, (height, breadth, reach) in REACH.items():
                    if kind[0] != part:
                        continue
                    rows, columns = range(-reach, height + reach), range(-reach, breadth + reach)
                    if dr:
                        rows = rows[:reach] if dr < 0 else rows[-reach:]
                        columns = columns[reach:-reach]
                    else:
                        columns = columns[:reach] if dc < 0 else columns[-reach:]
                    for i in rows:
                        for j in columns:
                            source = COLUMN[(kind, i - dr * height, j - dc * breadth)]
                            cells.append((kind, i, j, source))
                message.append(cells + [None] * (-len(cells) % 8))
            plan.append(message)
            starts.append(at)
            at += len(message[0]) + len(message[1])
        for start, message in zip(starts[first:], plan[first:]):
            for n, cell in enumerate(message[0] + message[1]):
                if cell:
                    COLUMN[cell[:3]] = start + n
    return plan, starts, at


PLAN, MSG_AT, KNOWN = message_plan()
MSG_ROWS = [end - start for start, end in zip(MSG_AT, MSG_AT[1:] + [KNOWN])]
MSG_CUT = [len(message[0]) for message in PLAN]
SIDE_END = MSG_AT[2]
SEND_SIDE = np.zeros((SIDE_END - LOC, LOC), np.float32)
SEND_ENDS = np.zeros((KNOWN - SIDE_END, SIDE_END), np.float32)
for n_, message_ in enumerate(PLAN):
    for m_, cell_ in enumerate(message_[0] + message_[1]):
        if cell_ and n_ < 2:
            SEND_SIDE[MSG_AT[n_] - LOC + m_, cell_[3]] = 1.0
        elif cell_:
            SEND_ENDS[MSG_AT[n_] - SIDE_END + m_, cell_[3]] = 1.0

STACKED = {}
STACK_ROWS = []
for part_ in (0, 1):
    at_ = G1 + G2
    for kind_, (height_, breadth_, _) in REACH.items():
        if kind_[0] == "db"[part_]:
            for i_ in range(height_):
                for j_ in range(breadth_):
                    STACKED[(kind_, i_, j_)] = local_row(kind_, i_, j_) - part_ * (G1 + G2)
    for message_ in PLAN:
        for m_, cell_ in enumerate(message_[part_]):
            if cell_:
                STACKED[cell_[:3]] = at_ + m_
        at_ += len(message_[part_])
    STACK_ROWS.append(at_)

INNER = G1 + G2
QROW = {}
for i_ in range(H1):
    for j_ in range(W1):
        QROW[(1, i_, j_)] = rho(i_, j_)
for i_ in range(H2):
    for j_ in range(W2):
        QROW[(2, i_, j_)] = G1 + i_ * W2 + j_
next_ = INNER
for level_, (height_, breadth_) in ((1, (H1, W1)), (2, (H2, W2))):
    for i_ in range(-1, height_ + 1):
        for j_ in range(-1, breadth_ + 1):
            if (level_, i_, j_) not in QROW:
                QROW[(level_, i_, j_)] = next_
                next_ += 1
QROWS = -(-next_ // 16) * 16

TAP_AT = np.full((QROWS, STACK_ROWS[0]), -1, np.int32)
PICK_BACK = np.zeros((QROWS, STACK_ROWS[1]), np.float32)
TAP_BACK = np.full((INNER, QROWS), -1, np.int32)
for (level_, i_, j_), q_ in QROW.items():
    PICK_BACK[q_, STACKED[("b%d" % level_, i_, j_)]] = 1.0
    for a_ in (-1, 0, 1):
        for b_ in (-1, 0, 1):
            tap_ = (level_ - 1) * 9 + (a_ + 1) * 3 + b_ + 1
            TAP_AT[q_, STACKED[("d%d" % level_, i_ + a_, j_ + b_)]] = tap_
            if q_ < INNER:
                TAP_BACK[q_, QROW[(level_, i_ - a_, j_ - b_)]] = tap_


def split(value):
    high = value.astype(BF)
    return high, (value - high.astype(F32)).astype(BF)


def mm(left, right):
    return jnp.dot(left, right, preferred_element_type=F32)


def rows_forward(parts, bands=(0, 1)):
    plus = [parts[0][k] + parts[1][k] for k in range(K)]
    minus = [parts[0][k] - parts[1][k] for k in range(K)]
    out = []
    for band in bands:
        outs = []
        for m in range(K):
            total = None
            for k in range(K):
                first, second = BANK[band, m, 0, k], BANK[band, m, 1, k]
                if first == 0.0:
                    continue
                term = (plus if first * second > 0 else minus)[k] * float(first)
                total = term if total is None else total + term
            outs.append(total)
        out.append(outs)
    return out


def rows_inverse(parts, bands=(0, 1)):
    out = [[None] * K, [None] * K]
    for k in range(K):
        same, other = None, None
        for band in bands:
            for m in range(K):
                first, second = BANK[band, m, 0, k], BANK[band, m, 1, k]
                if first == 0.0:
                    continue
                term = parts[band][m] * float(first)
                if first * second > 0:
                    same = term if same is None else same + term
                else:
                    other = term if other is None else other + term
        out[0][k] = same + other if other is not None else same
        out[1][k] = same - other if other is not None else same
    return out


def quarter(index):
    return lax.broadcasted_iota(jnp.int32, (8, TILE), 1) // SUB == index


def pack_channels(first, second, out_ref):
    for n in range(F // TILE):
        lanes = slice(n * TILE, (n + 1) * TILE)
        sources = [first[:8, lanes], second[:8, lanes], first[8:, lanes], second[8:, lanes]]
        for s in range(TILE // SUB):
            total = None
            for t, source in enumerate(sources):
                moved = source if s == t else pltpu.roll(source, (t - s) % 4 * SUB, 1)
                total = moved if total is None else jnp.where(quarter(t), moved, total)
            out_ref[n * 4 + s] = total


def unpack_channels(ref):
    out = [[], []]
    for n in range(F // TILE):
        sources = [ref[n * 4 + s] for s in range(TILE // SUB)]
        found = []
        for t in range(4):
            total = None
            for s, source in enumerate(sources):
                moved = source if s == t else pltpu.roll(source, (s - t) % 4 * SUB, 1)
                total = moved if total is None else jnp.where(quarter(s), moved, total)
            found.append(total)
        out[0].append(jnp.concatenate([found[0], found[2]], axis=0))
        out[1].append(jnp.concatenate([found[1], found[3]], axis=0))
    return out


def analyze_kernel(field_ref, cot_ref, gather_ref, wh_ref, wl_ref, send_ref, loc_ref, up_ref, down_ref, part_ref):
    gather = gather_ref[...]
    lefts = [[], []]
    for source in (field_ref, cot_ref):
        moved = mm(gather, source[...]).astype(BF)
        for a in range(2):
            for k in range(K):
                for b in range(2):
                    at = (a * 2 + b) * G1
                    lefts[b].append(moved[at : at + G1, k * QW : (k + 1) * QW])
    left = [jnp.concatenate(part, axis=0) for part in lefts]
    high = mm(left[0], wh_ref[: 2 * CH * 2]) + mm(left[1], wh_ref[2 * CH * 2 :])
    low = mm(left[0], wl_ref[: 2 * CH * 2]) + mm(left[1], wl_ref[2 * CH * 2 :])
    mixed = high + low
    lefts = [[], []]
    locs = []
    for n in range(2):
        parts = [[mixed[((n * 2 + a) * K + k) * G1 :][:G1] for k in range(K)] for a in range(2)]
        out = rows_forward(parts)
        detail = [out[0][m][:, QW:] for m in range(K)] + [out[1][m][:, :QW] for m in range(K)]
        detail += [out[1][m][:, QW:] for m in range(K)]
        locs.append(jnp.concatenate(detail, axis=1).astype(BF))
        for a in range(2):
            for k in range(K):
                for b in range(2):
                    at = (a * 2 + b) * G2
                    lefts[b].append(out[0][k][at : at + G2, :QW])
    mixed = None
    for b in range(2):
        high, low = split(jnp.concatenate(lefts[b], axis=0))
        rows = slice(b * QW, (b + 1) * QW)
        term = mm(high, wh_ref[rows]) + mm(low, wh_ref[rows]) + mm(high, wl_ref[rows])
        mixed = term if mixed is None else mixed + term
    coarse = []
    for n in range(2):
        parts = [[mixed[((n * 2 + a) * K + k) * G2 :][:G2] for k in range(K)] for a in range(2)]
        out = rows_forward(parts)
        detail = [out[0][m][:, QW:] for m in range(K)] + [out[1][m][:, :QW] for m in range(K)]
        detail += [out[1][m][:, QW:] for m in range(K)]
        at = n * INNER
        loc_ref[at : at + G1, :] = locs[n]
        loc_ref[at + G1 : at + INNER, :] = jnp.concatenate(detail, axis=1).astype(BF)
        coarse.append(jnp.concatenate([out[0][m][:, :QW] for m in range(K)], axis=1))
    pack_channels(*coarse, part_ref)
    part_ref.send()
    loc_ref.send()
    moved = mm(send_ref[...], loc_ref[...])
    up_ref[...] = moved[: MSG_ROWS[0]].astype(BF)
    down_ref[...] = moved[MSG_ROWS[0] :].astype(BF)


def stack(parts):
    return jnp.concatenate([part.astype(F32) for part in parts], axis=0).astype(BF)


def along_kernel(rows_ref, parts_ref, out_ref):
    high, low = split(parts_ref[...].reshape(-1, TILE))

    def times(n):
        left_high = rows_ref[n, 0]
        return mm(left_high, high) + mm(rows_ref[n, 1], high) + mm(left_high, low)

    near = lax.broadcasted_iota(jnp.int32, (4 * MODES, TILE), 1) < TILE // 2
    first = times(0) + pltpu.roll(times(1), TILE // 2, 1)
    second = pltpu.roll(times(2), TILE // 2, 1) + times(3)
    out = jnp.where(near, first, second).astype(BF)
    for n in range(out_ref.shape[0]):
        out_ref[n] = out


def ends_kernel(stencil_ref, send_ref, loc_ref, up_ref, down_ref, tap_ref, tap_back_ref, places_ref, gains_ref, left_ref, right_ref, lead_ref, lead_back_ref, my_ref):
    known = jnp.concatenate([loc_ref[...], stack([up_ref[...], down_ref[...]])], axis=0)
    moved = mm(send_ref[...], known).astype(BF)
    left_ref[...] = moved[: MSG_ROWS[2]]
    left_ref.send()
    right_ref[...] = moved[MSG_ROWS[2] :]
    right_ref.send()
    taps = [stencil_ref[n // 9, n // 3 % 3, n % 3] for n in range(18)]
    lead_ref[:QROWS], lead_ref[QROWS:] = split(tap_matrix(tap_ref[...], taps))
    lead_back_ref[:INNER], lead_back_ref[INNER:] = split(tap_matrix(tap_back_ref[...], taps))
    my_ref[2 * MODES * MODES :] = places_ref[...]
    gains = gains_ref[...]
    own = (lax.axis_index("row") * 2 + lax.axis_index("col") % 2) % 4
    group = lax.broadcasted_iota(jnp.int32, gains.shape, 1) // SUB
    total = jnp.zeros_like(gains)
    for s in range(4):
        for t in range(2):
            moved = pltpu.roll(gains, (t - s) % 4 * SUB, 1) if s != t else gains
            total = jnp.where((group == t) & (own == s), moved, total)
    my_ref[: 2 * MODES * MODES] = total


def modes_kernel(scale, across_ref, rows_ref, my_ref, parts_ref, out_ref):
    parts = parts_ref[...].reshape(-1, TILE)
    half = TILE // 2
    modes = mm(across_ref[0, 0], parts) + mm(across_ref[0, 1], parts)
    modes = modes + pltpu.roll(mm(across_ref[1, 0], parts) + mm(across_ref[1, 1], parts), half, 1)
    count = modes.shape[0]
    coeffs = split(my_ref[:count] * modes * scale)
    near = lax.broadcasted_iota(jnp.int32, (4 * MODES, TILE), 1) < half
    wide = []
    for core in range(2):
        high, low = split(my_ref[count + core * 4 * MODES : count + (core + 1) * 4 * MODES])
        wide.append(mm(high, coeffs[0]) + mm(high, coeffs[1]) + mm(low, coeffs[0]))
    wide = jnp.where(near, wide[0], pltpu.roll(wide[1], half, 1))
    first, second = mm3(rows_ref.at[0], wide), mm3(rows_ref.at[1], wide)
    near = lax.broadcasted_iota(jnp.int32, first.shape, 1) < half
    shape = (out_ref.shape[0], 8, TILE)
    out_ref[:, 0] = jnp.where(near, first, pltpu.roll(second, half, 1)).reshape(shape)
    out_ref[:, 1] = jnp.where(near, pltpu.roll(first, half, 1), second).reshape(shape)


def mm3(left_ref, right):
    high, low = split(right)
    left_high = left_ref[0]
    return mm(left_high, high) + mm(left_ref[1], high) + mm(left_high, low)


def tap_matrix(at, taps):
    total = jnp.zeros(at.shape, F32)
    for n, tap in enumerate(taps):
        total = jnp.where(at == n, tap, total)
    return total


def detail_kernel(lead_ref, pick_ref, loc_ref, up_ref, down_ref, left_ref, right_ref, mix_ref, lead_back_ref, filter_ref, scatter_ref, out_ref, scratch):
    messages = [ref[...].astype(F32) for ref in (up_ref, down_ref, left_ref, right_ref)]
    details = [message[:cut] for message, cut in zip(messages, MSG_CUT)]
    others = [message[cut:] for message, cut in zip(messages, MSG_CUT)]
    details = jnp.concatenate([loc_ref[:INNER], stack(details)], axis=0)
    others = jnp.concatenate([loc_ref[INNER:], stack(others)], axis=0)
    lead, pick, lead_back = lead_ref[...], pick_ref[...], lead_back_ref[...]
    slope = math.sqrt(2.0 / math.pi)
    acts, derivatives, backs = [], [], []
    for band in range(3):
        lanes = slice(band * F, (band + 1) * F)
        found = mm(lead, details[:, lanes])
        pre = found[:QROWS] + found[QROWS:]
        square = pre * pre
        curve = jnp.tanh(slope * (pre + 0.044715 * (pre * square)))
        cdf = 0.5 * (1.0 + curve)
        acts.append((pre * cdf)[:INNER].astype(BF))
        derivatives.append(
            cdf + (0.5 * slope) * pre * (1.0 - curve * curve) * (1.0 + (3 * 0.044715) * square)
        )
        backs.append(mm(pick, others[:, lanes]).astype(BF))
    mix = mix_ref[...]
    mixed = mm(jnp.concatenate(acts, axis=0), mix)
    back = lax.dot_general(
        jnp.concatenate(backs, axis=0), mix, (((1,), (1,)), ((), ())), preferred_element_type=F32
    )
    for band in range(3):
        scratch[0, band] = mixed[band * INNER : (band + 1) * INNER].astype(BF)
        grad = (back[band * QROWS : (band + 1) * QROWS] * derivatives[band]).astype(BF)
        found = mm(lead_back, grad)
        scratch[1, band] = (found[:INNER] + found[INNER:]).astype(BF)
    found = synthesize(None, scratch, slice(G1, INNER), filter_ref)
    found = synthesize([[part.astype(BF) for part in place(out)] for out in found], scratch, slice(0, G1), filter_ref)
    scatter = scatter_ref[...]
    for n in range(2):
        for k, block in enumerate(place(found[n])):
            out_ref[n, :, k * QW : (k + 1) * QW] = mm(scatter, block.astype(BF)).astype(BF)


def finish_kernel(filter_ref, left_ref, part_ref, coarse_ref, up_ref, down_ref):
    count = K * G2
    tiles = unpack_channels(coarse_ref)
    states = [
        [jnp.concatenate(own[2 * m : 2 * m + 2], axis=1) for m in range(K)] for own in tiles
    ]
    wide = mm(jnp.concatenate(states[0] + states[1], axis=0).astype(BF), filter_ref[...]).astype(BF)
    for n, ref in enumerate((up_ref, down_ref)):
        rows = wide[n * count : (n + 1) * count]
        right = jnp.concatenate([rows[:, j * QW : (j + 1) * QW] for j in range(4)], axis=0)
        for k in range(K):
            lanes = slice(k * QW, (k + 1) * QW)
            found = mm(left_ref[k], right)
            ref[:, lanes] = (part_ref[n, :, lanes] + found).astype(BF)
        ref.send()


def synthesize(states, scratch, rows, filter_ref):
    lefts = []
    for n in range(2):
        for band in range(2):
            for m in range(K):
                lanes = slice(m * QW, (m + 1) * QW)
                pair = [scratch[n, 1, rows, lanes], scratch[n, 2, rows, lanes]]
                if band == 0:
                    detail = scratch[n, 0, rows, lanes]
                    pair = [jnp.zeros_like(detail) if states is None else states[n][m], detail]
                lefts.append(jnp.concatenate(pair, axis=1))
    left = jnp.concatenate(lefts, axis=0)
    wide = mm(left, filter_ref[...])
    count = rows.stop - rows.start
    out = []
    for n in range(2):
        parts = [[wide[((n * 2 + band) * K + m) * count :][:count] for m in range(K)] for band in range(2)]
        out.append(rows_inverse(parts))
    return out


def times_filter(left, high_filter, low_filter):
    high, low = split(left)
    return mm(high, high_filter) + mm(low, high_filter) + mm(high, low_filter)


def place(out):
    return [
        jnp.concatenate(
            [out[a][k][:, b * QW : (b + 1) * QW] for a in range(2) for b in range(2)], axis=0
        )
        for k in range(K)
    ]


def mode_tables(row_count, chip_count):
    freqs = np.arange(MODES)
    angle = 2.0 * np.pi * np.outer(freqs, np.arange(row_count * H2)) / (row_count * H2)
    waves = np.stack([np.cos(angle), np.sin(angle)]).reshape(2, MODES, row_count, H2)
    rows = np.zeros((2, MODES, W2, row_count, G2))
    for i in range(H2):
        for j in range(W2):
            rows[:, :, j, :, i * W2 + j] = waves[:, :, :, i]
    rows = rows.reshape(2 * MODES * W2, row_count, 2, 8)
    back = rows.transpose(2, 1, 3, 0).reshape(2, row_count * 8, -1)
    along = np.zeros((2, 2, 2 * MODES * W2, row_count, 2, 8))
    for core in range(2):
        for half in range(2):
            along[core, half, :, :, core] = rows[:, :, half]
    along = along.reshape(4, 2 * MODES * W2, -1)
    angle = 2.0 * np.pi * np.outer(freqs, np.arange(chip_count * 2 * W2)) / (chip_count * 2 * W2)
    cosine, sine = [part.reshape(MODES, chip_count, 2, W2) for part in (np.cos(angle), np.sin(angle))]
    places = np.zeros((chip_count, 2, 2, MODES, MODES, 2, MODES, W2))
    for u in range(MODES):
        for v in range(MODES):
            places[:, :, 0, u, v, 0, u] = cosine[v]
            places[:, :, 0, u, v, 1, u] = -sine[v]
            places[:, :, 1, u, v, 0, u] = sine[v]
            places[:, :, 1, u, v, 1, u] = cosine[v]
    places = places.reshape(chip_count, 2, 2 * MODES * MODES, 2 * MODES * W2)
    across = places.transpose(1, 2, 0, 3).reshape(2, 2 * MODES * MODES, -1)
    places = places.transpose(0, 1, 3, 2).reshape(chip_count, 4 * MODES * W2, -1)
    found = [jnp.asarray(np.stack(halves(part), axis=part.ndim - 2)) for part in (along, back, across)]
    return found + [jnp.asarray(places.astype(np.float32))]


class Fetched:
    def __init__(self, source, scratch, sem):
        self.shape = scratch.shape
        self.ref = scratch
        self.copy = pltpu.make_async_copy(source, scratch, sem)
        self.copy.start()

    def arrived(self):
        if self.copy is not None:
            self.copy.wait()
            self.copy = None
        return self.ref

    def __getitem__(self, index):
        return self.arrived()[index]


class Returned:
    def __init__(self, target, scratch, sem):
        self.shape = scratch.shape
        self.ref = scratch
        self.copy = pltpu.make_async_copy(scratch, target, sem)
        self.started = False

    def __getitem__(self, index):
        return self.ref[index]

    def __setitem__(self, index, value):
        self.ref[index] = value

    def send(self):
        if not self.started:
            self.copy.start()
            self.started = True


def call(kernel, outs, ins, micros, smem=0, near=0, picks=None, near_out=False, scratch=(), limit=60):
    picks = picks or {}
    count, single = len(ins), not isinstance(outs, list)
    outs = [outs] if single else outs
    far = range(smem, count - near)
    blocks = [
        jax.eval_shape(lambda part, n=n: picks[n][0](part), ins[n]) if n in picks else ins[n] for n in far
    ]

    def wrapped(*refs):
        own = list(refs[:count])
        results = list(refs[count : count + len(outs)])
        rest = list(refs[count + len(outs) :])
        sems = rest.pop()
        for n, at in enumerate(far):
            source = picks[at][1](own[at]) if at in picks else own[at]
            own[at] = Fetched(source, rest.pop(0), sems.at[n])
        if not near_out:
            for n in range(len(outs)):
                results[n] = Returned(results[n], rest.pop(0), sems.at[len(far) + n])
        kernel(*own, *results, *rest)
        for operand in own:
            if isinstance(operand, Fetched):
                operand.arrived()
        if not near_out:
            for result in results:
                result.send()
            for result in results:
                result.copy.wait()

    where = [pltpu.SMEM] * smem + [pltpu.HBM] * len(far) + [pltpu.VMEM] * near
    inner = [pltpu.VMEM(block.shape, block.dtype) for block in blocks]
    if not near_out:
        inner += [pltpu.VMEM(out.shape, out.dtype) for out in outs]
    result = pl.pallas_call(
        wrapped,
        out_shape=outs,
        in_specs=[pl.BlockSpec(memory_space=space) for space in where],
        out_specs=[pl.BlockSpec(memory_space=pltpu.VMEM if near_out else pltpu.HBM) for _ in outs],
        scratch_shapes=inner + list(scratch) + [pltpu.SemaphoreType.DMA((len(far) + len(outs),))],
        compiler_params=pltpu.CompilerParams(vmem_limit_bytes=limit * 1024 * 1024),
        cost_estimate=pl.CostEstimate(
            flops=int(micros * 1.1e9), bytes_accessed=int(micros * 1e6), transcendentals=0
        ),
    )(*ins)
    return result[0] if single else result


def body(field, mix, stencil, spectral, cotangent):
    row_count, col_count = lax.axis_size("row"), lax.axis_size("col")
    wh, wl = [jnp.asarray(part) for part in halves(COL_FILTER)]
    wht = jnp.asarray(np.ascontiguousarray(halves(COL_FILTER)[0].T))
    gather, scatter, send_side, send_ends, pick = [
        jnp.asarray(np.ascontiguousarray(part).astype(ml_dtypes.bfloat16))
        for part in (gather_table(), gather_table().T, SEND_SIDE, SEND_ENDS, PICK_BACK)
    ]
    chip_count = col_count // 2
    along, back, across, places = mode_tables(row_count, chip_count)
    shape = jax.ShapeDtypeStruct

    def table(array):
        return jnp.asarray(np.ascontiguousarray(array))

    def shift(message, dr, dc):
        axis, step = ("row", dr) if dr else ("col", dc)
        count = lax.axis_size(axis)
        return lax.ppermute(message, axis, [(n, (n - step) % count) for n in range(count)])

    coarse_back = table(halves(COARSE_RIGHT)[0].T)
    left_back = table(halves(COARSE_LEFT)[0].transpose(0, 2, 1))
    plane = [
        [r * col_count + 2 * z + core for r in range(row_count) for core in range(2)]
        for z in range(chip_count)
    ]
    chips = [[2 * z + core for z in range(chip_count)] for core in range(2)]

    def over_plane(pieces):
        return lax.all_to_all(pieces, ("row", "col"), 0, 0, tiled=True, axis_index_groups=plane)

    loc, to_up, to_down, part = call(
        analyze_kernel,
        [shape((LOC, 3 * F), BF)]
        + [shape((count, 3 * F), BF) for count in MSG_ROWS[:2]]
        + [shape((2 * row_count, 8, TILE), F32)],
        (field.reshape(FI * FJ, F), cotangent.reshape(FI * FJ, F), gather, wh, wl, send_side),
        4,
    )
    part = over_plane(part)
    up, down = shift(to_up, *SIDES[0]), shift(to_down, *SIDES[1])
    part = call(
        along_kernel,
        shape((chip_count, 4 * MODES, TILE), BF),
        (along, part),
        1,
        near=2,
        near_out=True,
        limit=8,
    )
    part, loc = lax.optimization_barrier((part, loc))
    part = lax.all_to_all(part, "col", 0, 0, tiled=True, axis_index_groups=chips)
    to_left, to_right, lead, lead_back, mine = call(
        ends_kernel,
        [shape((count, 3 * F), BF) for count in MSG_ROWS[2:]]
        + [shape((2 * QROWS, STACK_ROWS[0]), BF), shape((2 * INNER, QROWS), BF)]
        + [shape((2 * MODES * MODES + places.shape[1], TILE), F32)],
        (stencil, send_ends, loc, up, down, jnp.asarray(TAP_AT), jnp.asarray(TAP_BACK), places,
         spectral.reshape(-1, F)),
        0.01,
        smem=1,
        picks={
            7: (lambda array: array[0], lambda ref: ref.at[lax.axis_index("col") // 2]),
            8: (
                lambda array: array[:, :TILE],
                lambda ref: ref.at[:, pl.ds(pl.multiple_of(lax.axis_index("row") // 2 * TILE, TILE), TILE)],
            ),
        },
    )
    left, right = shift(to_left, *SIDES[2]), shift(to_right, *SIDES[3])
    part = call(
        functools.partial(modes_kernel, 1.0 / math.sqrt(row_count * H2 * col_count * W2)),
        shape((row_count, 2, 8, TILE), F32),
        (across, back, mine, part),
        1,
        near=4,
        near_out=True,
        limit=8,
    )
    part, loc = lax.optimization_barrier((part, loc))
    part = over_plane(part.reshape(2 * row_count, 8, TILE))
    details = call(
        detail_kernel,
        shape((2, FI * FJ, F), BF),
        (lead, pick, loc, up, down, left, right, mix, lead_back, wht, scatter),
        7,
        scratch=[pltpu.VMEM((2, 3, INNER, F), BF)],
    )
    layer_out, grad_field = call(
        finish_kernel,
        [shape((FI * FJ, F), BF)] * 2,
        (coarse_back, left_back, details, part),
        3,
        near=1,
    )
    return layer_out.reshape(FI, FJ, F), grad_field.reshape(FI, FJ, F)


def solution(mesh):
    placed = (P("row", "col", None), P(), P(), P(), P("row", "col", None))
    return jax.shard_map(
        body,
        mesh=mesh,
        in_specs=placed,
        out_specs=(P("row", "col", None), P("row", "col", None)),
        check_vma=False,
    )
```

```python
import functools
import math

import jax
import jax.numpy as jnp
import ml_dtypes
import numpy as np
from jax import lax
from jax.experimental import pallas as pl
from jax.experimental.pallas import tpu as pltpu
from jax.sharding import PartitionSpec as P

CH = 64
K = 4
MODES = 8
F = 1024
BF = jnp.bfloat16
F32 = jnp.float32
QW = K * CH

FI, FJ = 24, 8
H1, W1 = 12, 4
H2, W2 = 6, 2
G1, G2 = 64, 16
SIDES = [(-1, 0), (1, 0), (0, -1), (0, 1)]


def shifted_legendre(order_count):
    length = order_count + 1
    polys = [np.zeros(length), np.zeros(length)]
    polys[0][0] = 1.0
    polys[1][0] = -1.0
    polys[1][1] = 2.0
    for degree in range(1, order_count):
        times_t = np.zeros(length)
        times_t[1:] = 2.0 * polys[degree][:-1]
        times_t = times_t - polys[degree]
        polys.append(((2.0 * degree + 1.0) * times_t - degree * polys[degree - 1]) / (degree + 1.0))
    return [np.sqrt(2.0 * degree + 1.0) * polys[degree] for degree in range(order_count)]


def integrate_product(first, second):
    total = 0.0
    for power_a in range(first.shape[0]):
        for power_b in range(second.shape[0]):
            total = total + first[power_a] * second[power_b] / (power_a + power_b + 1.0)
    return total


def two_scale(order_count):
    polys = shifted_legendre(order_count)
    length = polys[0].shape[0]
    left_half = np.zeros((order_count, order_count))
    right_half = np.zeros((order_count, order_count))
    for out_index in range(order_count):
        coeffs = polys[out_index]
        halved = np.array([coeffs[power] * 0.5**power for power in range(length)])
        moved = np.zeros(length)
        for power in range(length):
            for lower in range(power + 1):
                moved[lower] = moved[lower] + coeffs[power] * 0.5**power * math.comb(power, lower)
        for in_index in range(order_count):
            left_half[out_index, in_index] = integrate_product(halved, polys[in_index]) / np.sqrt(2.0)
            right_half[out_index, in_index] = integrate_product(moved, polys[in_index]) / np.sqrt(2.0)
    scaling_rows = np.concatenate([left_half, right_half], axis=1)
    vectors = [scaling_rows[out_index] for out_index in range(order_count)]
    wavelet_rows = []
    for out_index in range(order_count):
        vector = np.zeros(2 * order_count)
        vector[out_index] = 1.0
        vector[order_count + out_index] = -1.0
        for earlier in vectors:
            vector = vector - np.dot(earlier, vector) * earlier
        vector = vector / np.sqrt(np.dot(vector, vector))
        vectors.append(vector)
        wavelet_rows.append(vector)
    return np.stack([scaling_rows, np.stack(wavelet_rows)]).reshape(2, order_count, 2, order_count)


BANK = two_scale(K)
BANK[np.abs(BANK) < 1e-12] = 0.0


def halves(array):
    high = np.asarray(array, np.float32).astype(ml_dtypes.bfloat16)
    low = (np.asarray(array, np.float64) - high.astype(np.float64)).astype(ml_dtypes.bfloat16)
    return high, low


COL_FILTER = np.kron(BANK.transpose(2, 3, 0, 1).reshape(2 * K, 2 * K), np.eye(CH))


def rho(i, j):
    return ((i % 2) * 2 + j % 2) * G2 + (i // 2) * W2 + j // 2


def local_row(kind, i, j):
    if kind == "d1":
        return rho(i, j)
    if kind == "d2":
        return G1 + i * W2 + j
    if kind == "b1":
        return G1 + G2 + rho(i, j)
    return 2 * G1 + G2 + i * W2 + j


LOC = 2 * (G1 + G2)
REACH = {"d1": (H1, W1, 2), "d2": (H2, W2, 2), "b1": (H1, W1, 1), "b2": (H2, W2, 1)}


TWICE = np.einsum("pbm,mak->pbak", BANK[0], BANK[0]).reshape(K, 4, K)
COARSE_LEFT = np.zeros((K, 4, K, G2, FI * FJ))
for i_ in range(FI):
    for j_ in range(FJ):
        COARSE_LEFT[:, j_ % 4, :, (i_ // 4) * W2 + j_ // 4, i_ * FJ + j_] = TWICE[:, i_ % 4, :].T
COARSE_LEFT = COARSE_LEFT.reshape(K, 4 * K * G2, FI * FJ)
COARSE_RIGHT = np.kron(TWICE.transpose(1, 2, 0).reshape(4 * K, K), np.eye(CH))
SUB = 32
TILE = 128


def gather_table():
    table = np.zeros((4 * G1, FI * FJ), np.float32)
    for i in range(FI):
        for j in range(FJ):
            table[((i % 2) * 2 + j % 2) * G1 + rho(i // 2, j // 2), i * FJ + j] = 1.0
    return table


COLUMN = {}
for kind_, (height_, breadth_, _) in REACH.items():
    for i_ in range(height_):
        for j_ in range(breadth_):
            COLUMN[(kind_, i_, j_)] = local_row(kind_, i_, j_)


def message_plan():
    at, plan, starts = LOC, [], []
    for first in (0, 2):
        for dr, dc in SIDES[first : first + 2]:
            message = []
            for part in ("d", "b"):
                cells = []
                for kind, (height, breadth, reach) in REACH.items():
                    if kind[0] != part:
                        continue
                    rows, columns = range(-reach, height + reach), range(-reach, breadth + reach)
                    if dr:
                        rows = rows[:reach] if dr < 0 else rows[-reach:]
                        columns = columns[reach:-reach]
                    else:
                        columns = columns[:reach] if dc < 0 else columns[-reach:]
                    for i in rows:
                        for j in columns:
                            source = COLUMN[(kind, i - dr * height, j - dc * breadth)]
                            cells.append((kind, i, j, source))
                message.append(cells + [None] * (-len(cells) % 8))
            plan.append(message)
            starts.append(at)
            at += len(message[0]) + len(message[1])
        for start, message in zip(starts[first:], plan[first:]):
            for n, cell in enumerate(message[0] + message[1]):
                if cell:
                    COLUMN[cell[:3]] = start + n
    return plan, starts, at


PLAN, MSG_AT, KNOWN = message_plan()
MSG_ROWS = [end - start for start, end in zip(MSG_AT, MSG_AT[1:] + [KNOWN])]
MSG_CUT = [len(message[0]) for message in PLAN]
SIDE_END = MSG_AT[2]
SEND_SIDE = np.zeros((SIDE_END - LOC, LOC), np.float32)
SEND_ENDS = np.zeros((KNOWN - SIDE_END, SIDE_END), np.float32)
for n_, message_ in enumerate(PLAN):
    for m_, cell_ in enumerate(message_[0] + message_[1]):
        if cell_ and n_ < 2:
            SEND_SIDE[MSG_AT[n_] - LOC + m_, cell_[3]] = 1.0
        elif cell_:
            SEND_ENDS[MSG_AT[n_] - SIDE_END + m_, cell_[3]] = 1.0

STACKED = {}
STACK_ROWS = []
for part_ in (0, 1):
    at_ = G1 + G2
    for kind_, (height_, breadth_, _) in REACH.items():
        if kind_[0] == "db"[part_]:
            for i_ in range(height_):
                for j_ in range(breadth_):
                    STACKED[(kind_, i_, j_)] = local_row(kind_, i_, j_) - part_ * (G1 + G2)
    for message_ in PLAN:
        for m_, cell_ in enumerate(message_[part_]):
            if cell_:
                STACKED[cell_[:3]] = at_ + m_
        at_ += len(message_[part_])
    STACK_ROWS.append(at_)

INNER = G1 + G2
QROW = {}
for i_ in range(H1):
    for j_ in range(W1):
        QROW[(1, i_, j_)] = rho(i_, j_)
for i_ in range(H2):
    for j_ in range(W2):
        QROW[(2, i_, j_)] = G1 + i_ * W2 + j_
next_ = INNER
for level_, (height_, breadth_) in ((1, (H1, W1)), (2, (H2, W2))):
    for i_ in range(-1, height_ + 1):
        for j_ in range(-1, breadth_ + 1):
            if (level_, i_, j_) not in QROW:
                QROW[(level_, i_, j_)] = next_
                next_ += 1
QROWS = -(-next_ // 16) * 16

TAP_AT = np.full((QROWS, STACK_ROWS[0]), -1, np.int32)
PICK_BACK = np.zeros((QROWS, STACK_ROWS[1]), np.float32)
TAP_BACK = np.full((INNER, QROWS), -1, np.int32)
for (level_, i_, j_), q_ in QROW.items():
    PICK_BACK[q_, STACKED[("b%d" % level_, i_, j_)]] = 1.0
    for a_ in (-1, 0, 1):
        for b_ in (-1, 0, 1):
            tap_ = (level_ - 1) * 9 + (a_ + 1) * 3 + b_ + 1
            TAP_AT[q_, STACKED[("d%d" % level_, i_ + a_, j_ + b_)]] = tap_
            if q_ < INNER:
                TAP_BACK[q_, QROW[(level_, i_ - a_, j_ - b_)]] = tap_


def split(value):
    high = value.astype(BF)
    return high, (value - high.astype(F32)).astype(BF)


def mm(left, right):
    return jnp.dot(left, right, preferred_element_type=F32)


def rows_forward(parts, bands=(0, 1)):
    plus = [parts[0][k] + parts[1][k] for k in range(K)]
    minus = [parts[0][k] - parts[1][k] for k in range(K)]
    out = []
    for band in bands:
        outs = []
        for m in range(K):
            total = None
            for k in range(K):
                first, second = BANK[band, m, 0, k], BANK[band, m, 1, k]
                if first == 0.0:
                    continue
                term = (plus if first * second > 0 else minus)[k] * float(first)
                total = term if total is None else total + term
            outs.append(total)
        out.append(outs)
    return out


def rows_inverse(parts, bands=(0, 1)):
    out = [[None] * K, [None] * K]
    for k in range(K):
        same, other = None, None
        for band in bands:
            for m in range(K):
                first, second = BANK[band, m, 0, k], BANK[band, m, 1, k]
                if first == 0.0:
                    continue
                term = parts[band][m] * float(first)
                if first * second > 0:
                    same = term if same is None else same + term
                else:
                    other = term if other is None else other + term
        out[0][k] = same + other if other is not None else same
        out[1][k] = same - other if other is not None else same
    return out


def quarter(index):
    return lax.broadcasted_iota(jnp.int32, (8, TILE), 1) // SUB == index


def pack_channels(first, second, out_ref):
    for n in range(F // TILE):
        lanes = slice(n * TILE, (n + 1) * TILE)
        sources = [first[:8, lanes], second[:8, lanes], first[8:, lanes], second[8:, lanes]]
        for s in range(TILE // SUB):
            total = None
            for t, source in enumerate(sources):
                moved = source if s == t else pltpu.roll(source, (t - s) % 4 * SUB, 1)
                total = moved if total is None else jnp.where(quarter(t), moved, total)
            out_ref[n * 4 + s] = total


def unpack_channels(ref):
    out = [[], []]
    for n in range(F // TILE):
        sources = [ref[n * 4 + s] for s in range(TILE // SUB)]
        found = []
        for t in range(4):
            total = None
            for s, source in enumerate(sources):
                moved = source if s == t else pltpu.roll(source, (s - t) % 4 * SUB, 1)
                total = moved if total is None else jnp.where(quarter(s), moved, total)
            found.append(total)
        out[0].append(jnp.concatenate([found[0], found[2]], axis=0))
        out[1].append(jnp.concatenate([found[1], found[3]], axis=0))
    return out


def analyze_kernel(field_ref, cot_ref, gather_ref, wh_ref, wl_ref, send_ref, loc_ref, up_ref, down_ref, part_ref):
    gather = gather_ref[...]
    lefts = [[], []]
    for source in (field_ref, cot_ref):
        moved = mm(gather, source[...]).astype(BF)
        for a in range(2):
            for k in range(K):
                for b in range(2):
                    at = (a * 2 + b) * G1
                    lefts[b].append(moved[at : at + G1, k * QW : (k + 1) * QW])
    left = [jnp.concatenate(part, axis=0) for part in lefts]
    high = mm(left[0], wh_ref[: 2 * CH * 2]) + mm(left[1], wh_ref[2 * CH * 2 :])
    low = mm(left[0], wl_ref[: 2 * CH * 2]) + mm(left[1], wl_ref[2 * CH * 2 :])
    mixed = high + low
    lefts = [[], []]
    locs = []
    for n in range(2):
        parts = [[mixed[((n * 2 + a) * K + k) * G1 :][:G1] for k in range(K)] for a in range(2)]
        out = rows_forward(parts)
        detail = [out[0][m][:, QW:] for m in range(K)] + [out[1][m][:, :QW] for m in range(K)]
        detail += [out[1][m][:, QW:] for m in range(K)]
        locs.append(jnp.concatenate(detail, axis=1).astype(BF))
        for a in range(2):
            for k in range(K):
                for b in range(2):
                    at = (a * 2 + b) * G2
                    lefts[b].append(out[0][k][at : at + G2, :QW])
    mixed = None
    for b in range(2):
        high, low = split(jnp.concatenate(lefts[b], axis=0))
        rows = slice(b * QW, (b + 1) * QW)
        term = mm(high, wh_ref[rows]) + mm(low, wh_ref[rows]) + mm(high, wl_ref[rows])
        mixed = term if mixed is None else mixed + term
    coarse = []
    for n in range(2):
        parts = [[mixed[((n * 2 + a) * K + k) * G2 :][:G2] for k in range(K)] for a in range(2)]
        out = rows_forward(parts)
        detail = [out[0][m][:, QW:] for m in range(K)] + [out[1][m][:, :QW] for m in range(K)]
        detail += [out[1][m][:, QW:] for m in range(K)]
        at = n * INNER
        loc_ref[at : at + G1, :] = locs[n]
        loc_ref[at + G1 : at + INNER, :] = jnp.concatenate(detail, axis=1).astype(BF)
        coarse.append(jnp.concatenate([out[0][m][:, :QW] for m in range(K)], axis=1))
    pack_channels(*coarse, part_ref)
    part_ref.send()
    loc_ref.send()
    moved = mm(send_ref[...], loc_ref[...])
    first, second = by_parity(moved[: MSG_ROWS[0]], moved[MSG_ROWS[0] :])
    up_ref[...] = first.astype(BF)
    down_ref[...] = second.astype(BF)


def by_parity(first, second):
    even = lax.axis_index("row") % 2 == 0
    return jnp.where(even, first, second), jnp.where(even, second, first)


def stack(parts):
    return jnp.concatenate([part.astype(F32) for part in parts], axis=0).astype(BF)


def along_kernel(rows_ref, parts_ref, out_ref):
    high, low = split(parts_ref[...].reshape(-1, TILE))

    def times(n):
        left_high = rows_ref[n, 0]
        return mm(left_high, high) + mm(rows_ref[n, 1], high) + mm(left_high, low)

    near = lax.broadcasted_iota(jnp.int32, (4 * MODES, TILE), 1) < TILE // 2
    first = times(0) + pltpu.roll(times(1), TILE // 2, 1)
    second = pltpu.roll(times(2), TILE // 2, 1) + times(3)
    out = jnp.where(near, first, second).astype(BF)
    for n in range(out_ref.shape[0]):
        out_ref[n] = out


def ends_kernel(stencil_ref, send_ref, loc_ref, up_ref, down_ref, tap_ref, tap_back_ref, places_ref, gains_ref, left_ref, right_ref, lead_ref, lead_back_ref, my_ref):
    down, up = by_parity(up_ref[...].astype(F32), down_ref[...].astype(F32))
    known = jnp.concatenate([loc_ref[...], stack([up, down])], axis=0)
    moved = mm(send_ref[...], known).astype(BF)
    left_ref[...] = moved[: MSG_ROWS[2]]
    left_ref.send()
    right_ref[...] = moved[MSG_ROWS[2] :]
    right_ref.send()
    taps = [stencil_ref[n // 9, n // 3 % 3, n % 3] for n in range(18)]
    lead_ref[:QROWS], lead_ref[QROWS:] = split(tap_matrix(tap_ref[...], taps))
    lead_back_ref[:INNER], lead_back_ref[INNER:] = split(tap_matrix(tap_back_ref[...], taps))
    my_ref[2 * MODES * MODES :] = places_ref[...]
    gains = gains_ref[...]
    own = (lax.axis_index("row") * 2 + lax.axis_index("col") % 2) % 4
    group = lax.broadcasted_iota(jnp.int32, gains.shape, 1) // SUB
    total = jnp.zeros_like(gains)
    for s in range(4):
        for t in range(2):
            moved = pltpu.roll(gains, (t - s) % 4 * SUB, 1) if s != t else gains
            total = jnp.where((group == t) & (own == s), moved, total)
    my_ref[: 2 * MODES * MODES] = total


def modes_kernel(scale, across_ref, rows_ref, my_ref, parts_ref, out_ref):
    parts = parts_ref[...].reshape(-1, TILE)
    half = TILE // 2
    modes = mm(across_ref[0, 0], parts) + mm(across_ref[0, 1], parts)
    modes = modes + pltpu.roll(mm(across_ref[1, 0], parts) + mm(across_ref[1, 1], parts), half, 1)
    count = modes.shape[0]
    coeffs = split(my_ref[:count] * modes * scale)
    near = lax.broadcasted_iota(jnp.int32, (4 * MODES, TILE), 1) < half
    wide = []
    for core in range(2):
        high, low = split(my_ref[count + core * 4 * MODES : count + (core + 1) * 4 * MODES])
        wide.append(mm(high, coeffs[0]) + mm(high, coeffs[1]) + mm(low, coeffs[0]))
    wide = jnp.where(near, wide[0], pltpu.roll(wide[1], half, 1))
    first, second = mm3(rows_ref.at[0], wide), mm3(rows_ref.at[1], wide)
    near = lax.broadcasted_iota(jnp.int32, first.shape, 1) < half
    shape = (out_ref.shape[0], 8, TILE)
    out_ref[:, 0] = jnp.where(near, first, pltpu.roll(second, half, 1)).reshape(shape)
    out_ref[:, 1] = jnp.where(near, pltpu.roll(first, half, 1), second).reshape(shape)


def mm3(left_ref, right):
    high, low = split(right)
    left_high = left_ref[0]
    return mm(left_high, high) + mm(left_ref[1], high) + mm(left_high, low)


def tap_matrix(at, taps):
    total = jnp.zeros(at.shape, F32)
    for n, tap in enumerate(taps):
        total = jnp.where(at == n, tap, total)
    return total


def detail_kernel(lead_ref, pick_ref, loc_ref, up_ref, down_ref, left_ref, right_ref, mix_ref, lead_back_ref, filter_ref, scatter_ref, out_ref, scratch):
    messages = [ref[...].astype(F32) for ref in (up_ref, down_ref, left_ref, right_ref)]
    messages[:2] = by_parity(*messages[:2])[::-1]
    details = [message[:cut] for message, cut in zip(messages, MSG_CUT)]
    others = [message[cut:] for message, cut in zip(messages, MSG_CUT)]
    details = jnp.concatenate([loc_ref[:INNER], stack(details)], axis=0)
    others = jnp.concatenate([loc_ref[INNER:], stack(others)], axis=0)
    lead, pick, lead_back = lead_ref[...], pick_ref[...], lead_back_ref[...]
    slope = math.sqrt(2.0 / math.pi)
    acts, derivatives, backs = [], [], []
    for band in range(3):
        lanes = slice(band * F, (band + 1) * F)
        found = mm(lead, details[:, lanes])
        pre = found[:QROWS] + found[QROWS:]
        square = pre * pre
        curve = jnp.tanh(slope * (pre + 0.044715 * (pre * square)))
        cdf = 0.5 * (1.0 + curve)
        acts.append((pre * cdf)[:INNER].astype(BF))
        derivatives.append(
            cdf + (0.5 * slope) * pre * (1.0 - curve * curve) * (1.0 + (3 * 0.044715) * square)
        )
        backs.append(mm(pick, others[:, lanes]).astype(BF))
    mix = mix_ref[...]
    mixed = mm(jnp.concatenate(acts, axis=0), mix)
    back = lax.dot_general(
        jnp.concatenate(backs, axis=0), mix, (((1,), (1,)), ((), ())), preferred_element_type=F32
    )
    for band in range(3):
        scratch[0, band] = mixed[band * INNER : (band + 1) * INNER].astype(BF)
        grad = (back[band * QROWS : (band + 1) * QROWS] * derivatives[band]).astype(BF)
        found = mm(lead_back, grad)
        scratch[1, band] = (found[:INNER] + found[INNER:]).astype(BF)
    found = synthesize(None, scratch, slice(G1, INNER), filter_ref)
    found = synthesize([[part.astype(BF) for part in place(out)] for out in found], scratch, slice(0, G1), filter_ref)
    scatter = scatter_ref[...]
    for n in range(2):
        for k, block in enumerate(place(found[n])):
            out_ref[n, :, k * QW : (k + 1) * QW] = mm(scatter, block.astype(BF)).astype(BF)


def finish_kernel(filter_ref, left_ref, part_ref, coarse_ref, up_ref, down_ref):
    count = K * G2
    tiles = unpack_channels(coarse_ref)
    states = [
        [jnp.concatenate(own[2 * m : 2 * m + 2], axis=1) for m in range(K)] for own in tiles
    ]
    wide = mm(jnp.concatenate(states[0] + states[1], axis=0).astype(BF), filter_ref[...]).astype(BF)
    for n, ref in enumerate((up_ref, down_ref)):
        rows = wide[n * count : (n + 1) * count]
        right = jnp.concatenate([rows[:, j * QW : (j + 1) * QW] for j in range(4)], axis=0)
        for k in range(K):
            lanes = slice(k * QW, (k + 1) * QW)
            found = mm(left_ref[k], right)
            ref[:, lanes] = (part_ref[n, :, lanes] + found).astype(BF)
        ref.send()


def synthesize(states, scratch, rows, filter_ref):
    lefts = []
    for n in range(2):
        for band in range(2):
            for m in range(K):
                lanes = slice(m * QW, (m + 1) * QW)
                pair = [scratch[n, 1, rows, lanes], scratch[n, 2, rows, lanes]]
                if band == 0:
                    detail = scratch[n, 0, rows, lanes]
                    pair = [jnp.zeros_like(detail) if states is None else states[n][m], detail]
                lefts.append(jnp.concatenate(pair, axis=1))
    left = jnp.concatenate(lefts, axis=0)
    wide = mm(left, filter_ref[...])
    count = rows.stop - rows.start
    out = []
    for n in range(2):
        parts = [[wide[((n * 2 + band) * K + m) * count :][:count] for m in range(K)] for band in range(2)]
        out.append(rows_inverse(parts))
    return out


def times_filter(left, high_filter, low_filter):
    high, low = split(left)
    return mm(high, high_filter) + mm(low, high_filter) + mm(high, low_filter)


def place(out):
    return [
        jnp.concatenate(
            [out[a][k][:, b * QW : (b + 1) * QW] for a in range(2) for b in range(2)], axis=0
        )
        for k in range(K)
    ]


def mode_tables(row_count, chip_count):
    freqs = np.arange(MODES)
    angle = 2.0 * np.pi * np.outer(freqs, np.arange(row_count * H2)) / (row_count * H2)
    waves = np.stack([np.cos(angle), np.sin(angle)]).reshape(2, MODES, row_count, H2)
    rows = np.zeros((2, MODES, W2, row_count, G2))
    for i in range(H2):
        for j in range(W2):
            rows[:, :, j, :, i * W2 + j] = waves[:, :, :, i]
    rows = rows.reshape(2 * MODES * W2, row_count, 2, 8)
    back = rows.transpose(2, 1, 3, 0).reshape(2, row_count * 8, -1)
    along = np.zeros((2, 2, 2 * MODES * W2, row_count, 2, 8))
    for core in range(2):
        for half in range(2):
            along[core, half, :, :, core] = rows[:, :, half]
    along = along.reshape(4, 2 * MODES * W2, -1)
    angle = 2.0 * np.pi * np.outer(freqs, np.arange(chip_count * 2 * W2)) / (chip_count * 2 * W2)
    cosine, sine = [part.reshape(MODES, chip_count, 2, W2) for part in (np.cos(angle), np.sin(angle))]
    places = np.zeros((chip_count, 2, 2, MODES, MODES, 2, MODES, W2))
    for u in range(MODES):
        for v in range(MODES):
            places[:, :, 0, u, v, 0, u] = cosine[v]
            places[:, :, 0, u, v, 1, u] = -sine[v]
            places[:, :, 1, u, v, 0, u] = sine[v]
            places[:, :, 1, u, v, 1, u] = cosine[v]
    places = places.reshape(chip_count, 2, 2 * MODES * MODES, 2 * MODES * W2)
    across = places.transpose(1, 2, 0, 3).reshape(2, 2 * MODES * MODES, -1)
    places = places.transpose(0, 1, 3, 2).reshape(chip_count, 4 * MODES * W2, -1)
    found = [jnp.asarray(np.stack(halves(part), axis=part.ndim - 2)) for part in (along, back, across)]
    return found + [jnp.asarray(places.astype(np.float32))]


class Fetched:
    def __init__(self, source, scratch, sem):
        self.shape = scratch.shape
        self.ref = scratch
        self.copy = pltpu.make_async_copy(source, scratch, sem)
        self.copy.start()

    def arrived(self):
        if self.copy is not None:
            self.copy.wait()
            self.copy = None
        return self.ref

    def __getitem__(self, index):
        return self.arrived()[index]


class Returned:
    def __init__(self, target, scratch, sem):
        self.shape = scratch.shape
        self.ref = scratch
        self.copy = pltpu.make_async_copy(scratch, target, sem)
        self.started = False

    def __getitem__(self, index):
        return self.ref[index]

    def __setitem__(self, index, value):
        self.ref[index] = value

    def send(self):
        if not self.started:
            self.copy.start()
            self.started = True


def call(kernel, outs, ins, micros, smem=0, near=0, picks=None, near_out=False, scratch=(), limit=60):
    picks = picks or {}
    count, single = len(ins), not isinstance(outs, list)
    outs = [outs] if single else outs
    far = range(smem, count - near)
    blocks = [
        jax.eval_shape(lambda part, n=n: picks[n][0](part), ins[n]) if n in picks else ins[n] for n in far
    ]

    def wrapped(*refs):
        own = list(refs[:count])
        results = list(refs[count : count + len(outs)])
        rest = list(refs[count + len(outs) :])
        sems = rest.pop()
        for n, at in enumerate(far):
            source = picks[at][1](own[at]) if at in picks else own[at]
            own[at] = Fetched(source, rest.pop(0), sems.at[n])
        if not near_out:
            for n in range(len(outs)):
                results[n] = Returned(results[n], rest.pop(0), sems.at[len(far) + n])
        kernel(*own, *results, *rest)
        for operand in own:
            if isinstance(operand, Fetched):
                operand.arrived()
        if not near_out:
            for result in results:
                result.send()
            for result in results:
                result.copy.wait()

    where = [pltpu.SMEM] * smem + [pltpu.HBM] * len(far) + [pltpu.VMEM] * near
    inner = [pltpu.VMEM(block.shape, block.dtype) for block in blocks]
    if not near_out:
        inner += [pltpu.VMEM(out.shape, out.dtype) for out in outs]
    result = pl.pallas_call(
        wrapped,
        out_shape=outs,
        in_specs=[pl.BlockSpec(memory_space=space) for space in where],
        out_specs=[pl.BlockSpec(memory_space=pltpu.VMEM if near_out else pltpu.HBM) for _ in outs],
        scratch_shapes=inner + list(scratch) + [pltpu.SemaphoreType.DMA((len(far) + len(outs),))],
        compiler_params=pltpu.CompilerParams(vmem_limit_bytes=limit * 1024 * 1024),
        cost_estimate=pl.CostEstimate(
            flops=int(micros * 1.1e9), bytes_accessed=int(micros * 1e6), transcendentals=0
        ),
    )(*ins)
    return result[0] if single else result


def body(field, mix, stencil, spectral, cotangent):
    row_count, col_count = lax.axis_size("row"), lax.axis_size("col")
    wh, wl = [jnp.asarray(part) for part in halves(COL_FILTER)]
    wht = jnp.asarray(np.ascontiguousarray(halves(COL_FILTER)[0].T))
    gather, scatter, send_side, send_ends, pick = [
        jnp.asarray(np.ascontiguousarray(part).astype(ml_dtypes.bfloat16))
        for part in (gather_table(), gather_table().T, SEND_SIDE, SEND_ENDS, PICK_BACK)
    ]
    chip_count = col_count // 2
    along, back, across, places = mode_tables(row_count, chip_count)
    shape = jax.ShapeDtypeStruct

    def table(array):
        return jnp.asarray(np.ascontiguousarray(array))

    def shift(message, dr, dc):
        axis, step = ("row", dr) if dr else ("col", dc)
        count = lax.axis_size(axis)
        return lax.ppermute(message, axis, [(n, (n - step) % count) for n in range(count)])

    coarse_back = table(halves(COARSE_RIGHT)[0].T)
    left_back = table(halves(COARSE_LEFT)[0].transpose(0, 2, 1))
    plane = [
        [r * col_count + 2 * z + core for r in range(row_count) for core in range(2)]
        for z in range(chip_count)
    ]
    chips = [[2 * z + core for z in range(chip_count)] for core in range(2)]

    def over_plane(pieces):
        return lax.all_to_all(pieces, ("row", "col"), 0, 0, tiled=True, axis_index_groups=plane)

    loc, to_up, to_down, part = call(
        analyze_kernel,
        [shape((LOC, 3 * F), BF)]
        + [shape((count, 3 * F), BF) for count in MSG_ROWS[:2]]
        + [shape((2 * row_count, 8, TILE), F32)],
        (field.reshape(FI * FJ, F), cotangent.reshape(FI * FJ, F), gather, wh, wl, send_side),
        4,
    )
    part = over_plane(part)
    pairs = [(n, n ^ 1) for n in range(row_count)]
    up = lax.ppermute(to_up, "row", pairs)
    pairs = [(n, (n + 1 if n % 2 else n - 1) % row_count) for n in range(row_count)]
    down = lax.ppermute(to_down, "row", pairs)
    part = call(
        along_kernel,
        shape((chip_count, 4 * MODES, TILE), BF),
        (along, part),
        1,
        near=2,
        near_out=True,
        limit=8,
    )
    part, loc = lax.optimization_barrier((part, loc))
    part = lax.all_to_all(part, "col", 0, 0, tiled=True, axis_index_groups=chips)
    to_left, to_right, lead, lead_back, mine = call(
        ends_kernel,
        [shape((count, 3 * F), BF) for count in MSG_ROWS[2:]]
        + [shape((2 * QROWS, STACK_ROWS[0]), BF), shape((2 * INNER, QROWS), BF)]
        + [shape((2 * MODES * MODES + places.shape[1], TILE), F32)],
        (stencil, send_ends, loc, up, down, jnp.asarray(TAP_AT), jnp.asarray(TAP_BACK), places,
         spectral.reshape(-1, F)),
        0.01,
        smem=1,
        picks={
            7: (lambda array: array[0], lambda ref: ref.at[lax.axis_index("col") // 2]),
            8: (
                lambda array: array[:, :TILE],
                lambda ref: ref.at[:, pl.ds(pl.multiple_of(lax.axis_index("row") // 2 * TILE, TILE), TILE)],
            ),
        },
    )
    left, right = shift(to_left, *SIDES[2]), shift(to_right, *SIDES[3])
    part = call(
        functools.partial(modes_kernel, 1.0 / math.sqrt(row_count * H2 * col_count * W2)),
        shape((row_count, 2, 8, TILE), F32),
        (across, back, mine, part),
        1,
        near=4,
        near_out=True,
        limit=8,
    )
    part, loc = lax.optimization_barrier((part, loc))
    part = over_plane(part.reshape(2 * row_count, 8, TILE))
    details = call(
        detail_kernel,
        shape((2, FI * FJ, F), BF),
        (lead, pick, loc, up, down, left, right, mix, lead_back, wht, scatter),
        7,
        scratch=[pltpu.VMEM((2, 3, INNER, F), BF)],
    )
    layer_out, grad_field = call(
        finish_kernel,
        [shape((FI * FJ, F), BF)] * 2,
        (coarse_back, left_back, details, part),
        3,
        near=1,
    )
    return layer_out.reshape(FI, FJ, F), grad_field.reshape(FI, FJ, F)


def solution(mesh):
    placed = (P("row", "col", None), P(), P(), P(), P("row", "col", None))
    return jax.shard_map(
        body,
        mesh=mesh,
        in_specs=placed,
        out_specs=(P("row", "col", None), P("row", "col", None)),
        check_vma=False,
    )
```
